512 devices in a mesh: col: 64 (over z, y_hi, core), row: 8 (over y_lo, x).
Axes of the slice: x: 4, y: 8 (y_hi: 4, y_lo: 2; y = y_hi * 2 + y_lo), z: 8, core: 2. Of those that a mesh axis runs over, the one named last changes fastest.
Arguments:
- decoded: bfloat16 [3, 256, 8192], P(None, 'row', 'col'), may hold values from -6 to 6
- loop_in: bfloat16 [9, 32, 3], replicated, may hold values from -1.25 to 1.25
- loop_out: bfloat16 [9, 3, 32], replicated, may hold values from -0.375 to 0.375
- first_conv: bfloat16 [9, 64, 3], replicated, may hold values from -1.25 to 1.25
- dense_first: bfloat16 [9, 32, 64], replicated, may hold values from -0.25 to 0.25
- dense_second: bfloat16 [9, 32, 96], replicated, may hold values from -0.21875 to 0.21875
- dense_third: bfloat16 [9, 32, 128], replicated, may hold values from -0.1875 to 0.1875
- dense_fourth: bfloat16 [9, 32, 160], replicated, may hold values from -0.15625 to 0.15625
- dense_fifth: bfloat16 [9, 64, 192], replicated, may hold values from -0.15625 to 0.15625
- head_conv: bfloat16 [9, 12, 64], replicated, may hold values from -0.25 to 0.25
Outputs:
- upscaled: float32 [8, 64, 3, 16384], P('row', 'col')
The draws below stay inside these ranges and needn't reach their ends.
All inputs are finite; a program needn't handle non-finite values.
Results may differ from the reference program's by a relative error of at most 0.005.
Values may be sent and summed in bfloat16 or wider, within the bound.
No kernel may reach another device: no remote copies, remote signals or barrier semaphores. Data moves between devices by JAX's collectives and lax.ppermute only.
A program may use at most 128 MiB of HBM per device.

```python
import jax
import jax.numpy as jnp
from jax import lax

CHANNELS = 3
LF = 32
NF = 64
GC = 32
BH = 32
BW = 128
H = 256
W = 8192
N_COL = 64
N_ROW = 8


def block_levels(stream_key, dims, shards, least, top_value):
    loudness, own = 1.0, jax.random.fold_in(stream_key, 6)
    for axis_at, shards_of in shards:
        draws = jnp.exp(jax.random.uniform(jax.random.fold_in(own, axis_at), (shards_of,), jnp.float32, least / len(shards), top_value / len(shards)))
        loudness = loudness * jnp.repeat(draws, dims[axis_at] // shards_of).reshape([-1 if axis == axis_at else 1 for axis in range(len(dims))])
    return loudness


def normal_values(stream_key, shape, scale, limit, shards=(), kind=jnp.bfloat16):
    values = jax.random.normal(stream_key, shape, jnp.float32) * scale
    if len(shards) > 0:
        values = block_levels(stream_key, shape, shards, -0.22, 0.18) * values
    return jnp.clip(values, min=-limit, max=limit).astype(kind)


def setup_inputs(seed: int = 0) -> dict:
    arg_keys = jax.random.split(jax.random.key(seed), 11)
    return {
        "decoded": normal_values(arg_keys[0], (CHANNELS, H, W), 1.0, 6.0, ((1, 8), (2, 64))),
        "loop_in": normal_values(arg_keys[1], (9, LF, CHANNELS), (9 * CHANNELS) ** -0.5, 1.25),
        "loop_out": normal_values(arg_keys[2], (9, CHANNELS, LF), (9 * LF) ** -0.5, 0.375),
        "first_conv": normal_values(arg_keys[3], (9, NF, CHANNELS), (9 * CHANNELS) ** -0.5, 1.25),
        "dense_first": normal_values(arg_keys[4], (9, GC, NF), (9 * NF) ** -0.5, 0.25),
        "dense_second": normal_values(arg_keys[5], (9, GC, NF + GC), (9 * (NF + GC)) ** -0.5, 0.21875),
        "dense_third": normal_values(arg_keys[6], (9, GC, NF + 2 * GC), (9 * (NF + 2 * GC)) ** -0.5, 0.1875),
        "dense_fourth": normal_values(arg_keys[7], (9, GC, NF + 3 * GC), (9 * (NF + 3 * GC)) ** -0.5, 0.15625),
        "dense_fifth": normal_values(arg_keys[8], (9, NF, NF + 4 * GC), (9 * (NF + 4 * GC)) ** -0.5, 0.15625),
        "head_conv": normal_values(arg_keys[9], (9, 4 * CHANNELS, NF), (9 * NF) ** -0.5, 0.25),
    }


margin_cells = 9


def leaky_relu(values):
    return jnp.where(values >= 0, values, 0.2 * values)


def conv_valid(padded, weight):
    kernel = weight.reshape(3, 3, weight.shape[1], weight.shape[2]).transpose(2, 3, 0, 1)
    result = lax.conv_general_dilated(padded[None], kernel, (1, 1), "VALID", dimension_numbers=("NCHW", "OIHW", "NCHW"), preferred_element_type=jnp.float32)
    return result[0]


def conv_pieces(pieces, weight):
    summed = None
    offset = 0
    for member in pieces:
        channels = member.shape[0]
        term = conv_valid(member, weight[:, :, offset:offset + channels])
        summed = term if summed is None else summed + term
        offset = offset + channels
    return summed


def network(decoded, weights, prepare, clip_frame):
    loop_in, loop_out, first_conv, dense_list, head_conv = weights
    hidden = clip_frame(leaky_relu(conv_pieces([prepare(decoded)], loop_in))).astype(jnp.bfloat16)
    filtered = clip_frame(decoded.astype(jnp.float32) + conv_pieces([prepare(hidden)], loop_out)).astype(jnp.bfloat16)
    features = clip_frame(conv_pieces([prepare(filtered)], first_conv)).astype(jnp.bfloat16)
    pieces = [prepare(features)]
    for layer in range(4):
        dense_out = clip_frame(leaky_relu(conv_pieces(pieces, dense_list[layer]))).astype(jnp.bfloat16)
        pieces.append(prepare(dense_out))
    block_out = clip_frame(features.astype(jnp.float32) + 0.2 * conv_pieces(pieces, dense_list[4])).astype(jnp.bfloat16)
    return conv_pieces([prepare(block_out)], head_conv)


def pad_single(field):
    return jnp.pad(field, ((0, 0), (1, 1), (1, 1)))


def reference(decoded, loop_in, loop_out, first_conv, dense_first, dense_second, dense_third, dense_fourth, dense_fifth, head_conv):
    weights = (loop_in, loop_out, first_conv, (dense_first, dense_second, dense_third, dense_fourth, dense_fifth), head_conv)
    height = decoded.shape[1]
    width = decoded.shape[2]
    padded = jnp.pad(decoded, ((0, 0), (margin_cells, margin_cells), (margin_cells, margin_cells)))
    row_places = jnp.arange(height + 2 * margin_cells, dtype=jnp.int32)
    row_inside = (row_places >= margin_cells) & (row_places < margin_cells + height)

    def one_strip(strip_index):
        offset = (strip_index * BW).astype(jnp.int32)
        member = lax.dynamic_slice_in_dim(padded, offset, BW + 2 * margin_cells, axis=2)
        col_places = offset - margin_cells + jnp.arange(BW + 2 * margin_cells, dtype=jnp.int32)
        col_inside = (col_places >= 0) & (col_places < width)
        inside = (row_inside[:, None] & col_inside[None, :]).astype(jnp.float32)

        def clip_frame(values):
            return values * inside

        head_out = network(member, weights, pad_single, clip_frame)
        return head_out[:, margin_cells:margin_cells + height, margin_cells:margin_cells + BW]

    heads = lax.map(one_strip, jnp.arange(N_COL, dtype=jnp.int32))
    doubled = heads.reshape(N_COL, CHANNELS, 2, 2, height, BW).transpose(1, 4, 2, 0, 5, 3)
    doubled = doubled.reshape(CHANNELS, 2 * height, 2 * width)
    return doubled.reshape(CHANNELS, N_ROW, 2 * BH, 2 * width).transpose(1, 2, 0, 3)
```

```python
import jax
import jax.numpy as jnp
from jax import lax
from jax.experimental import pallas as pl
from jax.experimental.pallas import tpu as pltpu
from jax.sharding import PartitionSpec as P

BF = jnp.bfloat16
F32 = jnp.float32

STRIDE = 147
BASE = 128
PAIRS = 26
LANES = 4096
STEP = 256
HALO = 9
SOURCE = ((1, -1), (0, 0), (1, 0), (0, 1))


def shift_of(pair, tap):
    return pair * STRIDE + tap - 1


def tiles_of(layer):
    first = (layer + 1) // 2
    last = (50 - layer) // 2
    low = (BASE + first * STRIDE) // 128 * 128
    high = BASE + (last + 1) * STRIDE
    return range(low, high, STEP)


def iota(shape, dim):
    return lax.broadcasted_iota(jnp.int32, shape, dim)


def place_at(pair, phase):
    return 2 * pair + phase + 1


def picking(rows, depth, entries):
    return jnp.where(entries(iota((rows, depth), 0), iota((rows, depth), 1)), 1.0, 0.0).astype(BF)


def quotient(values, by):
    return lax.shift_right_arithmetic(values * (65536 // by + 1), 16)


def prep_kernel(
    loop_in, loop_out, first_conv, d1, d2, d3, d4, d5, head,
    w_in, w_out, w_first, w_f, w_1, w_2, w_3, w_4, w_head,
):
    for source, target in ((loop_in, w_in), (first_conv, w_first)):
        outs = source.shape[2]
        blank = jnp.zeros((1, outs), F32)
        flat = jnp.concatenate(
            [piece for t in range(9) for piece in (source[t].astype(F32), blank)], axis=0
        ).astype(BF)
        sides = []
        for p in range(2):

            def entries(m, k):
                group = lax.shift_right_arithmetic(m, 3)
                pair = quotient(group, 3)
                tap = group - 3 * pair
                down = 2 * pair - 1 + (lax.shift_right_arithmetic(m, 2) & 1) - p
                ok = (down >= 0) & (down <= 2) & ((m & 3) < 3)
                return ok & (k == (down * 3 + tap) * 4 + (m & 3))

            sides.append(jnp.dot(picking(72, 36, entries), flat, preferred_element_type=F32))
        target[...] = jnp.concatenate(sides, axis=1).T.astype(BF)
    blank = jnp.zeros((1, 32), F32)
    flat = jnp.concatenate(
        [piece for t in range(9) for piece in (loop_out[t].astype(F32), blank)], axis=0
    ).astype(BF)
    sides = []
    for q in range(2):

        def entries(m, k):
            group = lax.shift_right_arithmetic(m, 3)
            pair = quotient(group, 3)
            tap = group - 3 * pair
            down = 2 * pair - 1 + q - (lax.shift_right_arithmetic(m, 2) & 1)
            ok = (down >= 0) & (down <= 2) & ((m & 3) < 3)
            return ok & (k == (down * 3 + tap) * 4 + (m & 3))

        sides.append(jnp.dot(picking(72, 36, entries), flat, preferred_element_type=F32))
    w_out[...] = jnp.concatenate(sides, axis=1).astype(BF)
    blank = jnp.zeros((4, 64), F32)
    flat = jnp.concatenate(
        [piece for t in range(9) for piece in (head[t].astype(F32), blank)], axis=0
    ).astype(BF)
    sides = []
    for q in range(2):

        def entries(m, k):
            group = lax.shift_right_arithmetic(m, 5)
            pair = quotient(group, 3)
            tap = group - 3 * pair
            b = lax.shift_right_arithmetic(m, 4) & 1
            p = lax.shift_right_arithmetic(m, 3) & 1
            a = lax.shift_right_arithmetic(m, 2) & 1
            down = 2 * pair - 1 + q - p
            ok = (down >= 0) & (down <= 2) & ((m & 3) < 3)
            return ok & (k == (down * 3 + tap) * 16 + 4 * (m & 3) + 2 * a + b)

        sides.append(jnp.dot(picking(288, 144, entries), flat, preferred_element_type=F32))
    w_head[...] = jnp.concatenate(sides, axis=1).astype(BF)
    dense = (d1, d2, d3, d4, d5)
    for source, target in enumerate((w_f, w_1, w_2, w_3, w_4)):
        low = 0 if source == 0 else 32 + 32 * source
        ins = 64 if source == 0 else 32
        row = 0
        for weight in dense[source:]:
            outs = weight.shape[1]
            taps = [weight[t, :, low : low + ins] for t in range(9)]
            none = jnp.zeros((outs, 3 * ins), BF)
            joined = jnp.concatenate(taps, axis=1)
            target[row : row + outs, :] = jnp.concatenate([joined, none], axis=1)
            target[row + outs : row + 2 * outs, :] = jnp.concatenate([none, joined], axis=1)
            row += 2 * outs


def run_prep(*weights):
    vmem = pl.BlockSpec(memory_space=pltpu.VMEM)
    shapes = ((64, 72), (72, 64), (128, 72), (384, 768), (320, 384), (256, 384), (192, 384), (128, 384), (288, 128))
    return pl.pallas_call(
        prep_kernel,
        out_shape=[jax.ShapeDtypeStruct(shape, BF) for shape in shapes],
        in_specs=[vmem] * 9,
        out_specs=[vmem] * 9,
        compiler_params=pltpu.CompilerParams(vmem_limit_bytes=8 << 20),
        cost_estimate=pl.CostEstimate(flops=20_000_000, bytes_accessed=3_000_000, transcendentals=0),
        name="weights",
    )(*weights)


def lrelu(values):
    return jnp.maximum(values, 0.2 * values)


def main_kernel(
    place, ext, above, below, w_in, w_out, w_first, w_f, w_1, w_2, w_3, w_4, w_head,
    y_ref, x0, mask, hid, fil, xf, x1, x2, x3, x4, xb, acc, zs, hs,
):
    row_at = place[0]
    col_at = place[1]
    seam = col_at == 0
    for ref in (x0, hid, fil, xf, x1, x2, x3, x4, xb, zs):
        ref[...] = jnp.zeros(ref.shape, ref.dtype)

    lane = iota((8, LANES), 1) - BASE
    pair = lax.shift_right_arithmetic(lane * 28533, 22)
    column = lane - pair * STRIDE
    gap = jnp.logical_and(seam, column == 18)
    for phase in range(2):
        row = 2 * pair + phase - 1 - HALO + 32 * row_at
        keep = jnp.logical_and(jnp.logical_and(row >= 0, row < 256), jnp.logical_not(gap))
        mask[phase] = jnp.where(keep, 1.0, 0.0)

    def masked(values, phase, start):
        rows = values.shape[0]
        inside = mask[phase, :, start : start + STEP]
        return (values.reshape(rows // 8, 8, STEP) * inside[None]).reshape(rows, STEP)

    def wide(ref, plane):
        return jnp.concatenate([ref[0, plane], ref[1, plane]], axis=1)

    stacked = jnp.concatenate(
        [wide(ref, plane) for plane in range(3) for ref in (above, ext, below)], axis=0
    )
    rows = 8 * PAIRS
    m_at = iota((rows, 288), 0)
    k_at = iota((rows, 288), 1)
    stored = 2 * lax.shift_right_arithmetic(m_at, 3) + (lax.shift_right_arithmetic(m_at, 2) & 1)
    plane_at = m_at & 3
    pick = (plane_at < 3) & (stored >= 1) & (stored <= 50) & (k_at == plane_at * 96 + stored + 22)
    ordered = jnp.dot(
        jnp.where(pick, 1.0, 0.0).astype(BF), stacked, preferred_element_type=F32
    ).astype(BF)
    i_at = iota((256, 256), 0) - 110
    o_at = iota((256, 256), 1)
    late = jnp.logical_and(seam, o_at >= 18)
    wanted = jnp.where(late, o_at - 1, o_at)
    valid = (o_at < STRIDE) & jnp.logical_not(jnp.logical_and(seam, o_at == 18))
    place_cols = jnp.where((i_at == wanted) & valid, 1.0, 0.0).astype(BF)
    laid = jnp.dot(ordered, place_cols, preferred_element_type=F32)
    for g in range(PAIRS):
        x0[:, BASE + g * STRIDE : BASE + (g + 1) * STRIDE] = laid[8 * g : 8 * g + 8, :STRIDE]

    shifts = [(pair, tap) for pair in (-1, 0, 1) for tap in range(3)]

    def narrow_columns(ref, start):
        pieces = [
            ref[:, start + shift_of(pair, tap) : start + shift_of(pair, tap) + STEP]
            for pair, tap in shifts
        ]
        return jnp.concatenate(pieces, axis=0).astype(BF)

    for start in tiles_of(1):
        values = lrelu(jnp.dot(w_in[...], narrow_columns(x0, start), preferred_element_type=F32))
        for phase in range(2):
            part = slice(32 * phase, 32 * phase + 32)
            hid[part, start : start + STEP] = masked(values[part], phase, start).astype(BF)
    for start in tiles_of(1):
        zs[:, start : start + STEP] = jnp.dot(
            w_out[...], hid[:, start : start + STEP], preferred_element_type=F32
        )
    sub = iota((8, STEP), 0)
    for start in tiles_of(2):
        values = x0[:, start : start + STEP]
        for at, (pair_, tap) in enumerate(shifts):
            off = start + shift_of(pair_, tap)
            values = values + zs[8 * at : 8 * at + 8, off : off + STEP]
        inside = jnp.where(
            sub < 4, mask[0, :, start : start + STEP], mask[1, :, start : start + STEP]
        )
        fil[:, start : start + STEP] = (values * inside).astype(BF).astype(F32)

    for start in tiles_of(3):
        values = jnp.dot(w_first[...], narrow_columns(fil, start), preferred_element_type=F32)
        for phase in range(2):
            part = slice(64 * phase, 64 * phase + 64)
            xf[part, start : start + STEP] = masked(values[part], phase, start).astype(BF)

    def columns(ref, start):
        count = ref.shape[0] // 2
        pieces = []
        for phase, pair_ in SOURCE:
            for tap in range(3):
                off = start + shift_of(pair_, tap)
                pieces.append(ref[count * phase : count * (phase + 1), off : off + STEP])
        return jnp.concatenate(pieces, axis=0)

    for layer, (ref, weight, target) in enumerate(
        ((xf, w_f, x1), (x1, w_1, x2), (x2, w_2, x3), (x3, w_3, x4), (x4, w_4, xb))
    ):
        low = 64 * layer
        for start in tiles_of(4 + layer):
            span = slice(start, start + STEP)
            values = jnp.dot(weight[...], columns(ref, start), preferred_element_type=F32)
            if layer > 0:
                values = values + acc[low:, span]
            if layer < 4:
                acc[low + 64 :, span] = values[64:]
                values = lrelu(values[:64])
                count = 32
            else:
                values = xf[:, span].astype(F32) + 0.2 * values
                count = 64
            for phase in range(2):
                part = slice(count * phase, count * (phase + 1))
                target[part, span] = masked(values[part], phase, start).astype(BF)

    for start in tiles_of(8):
        hs[:, start : start + STEP] = jnp.dot(
            w_head[...], xb[:, start : start + STEP], preferred_element_type=F32
        )
    rows_out = []
    for g in range(5, 21):
        low = BASE + g * STRIDE
        values = None
        for at, (pair_, tap) in enumerate(shifts):
            off = low + shift_of(pair_, tap)
            term = hs[32 * at : 32 * at + 32, off : off + STEP]
            values = term if values is None else values + term
        rows_out.append(values.astype(BF))
    even = jnp.concatenate([values[:16] for values in rows_out], axis=0)
    odd = jnp.concatenate([values[16:] for values in rows_out], axis=0)
    k_at = iota((256, 256), 0)
    n_at = iota((256, 256), 1)
    cell = lax.shift_right_arithmetic(n_at, 1) + HALO
    cell = jnp.where(jnp.logical_and(seam, cell >= 18), cell + 1, cell)
    spread = [
        jnp.where((k_at == cell) & ((n_at & 1) == b), 1.0, 0.0).astype(BF) for b in range(2)
    ]
    result = jnp.dot(even, spread[0], preferred_element_type=F32) + jnp.dot(
        odd, spread[1], preferred_element_type=F32
    )
    first = result[:, :128].reshape(32, 8, 128)
    second = result[:, 128:].reshape(32, 8, 128)
    top = iota((32, 8, 128), 1) < 4
    even_rows = jnp.where(top, first, pltpu.roll(second, 4, 1)).astype(BF)
    odd_rows = jnp.where(top, pltpu.roll(first, 4, 1), second).astype(BF)
    for i in range(32):
        y_ref[2 * i] = even_rows[i]
        y_ref[2 * i + 1] = odd_rows[i]


def run_main(place, ext, above, below, weights):
    vmem = pl.BlockSpec(memory_space=pltpu.VMEM)
    return pl.pallas_call(
        main_kernel,
        out_shape=jax.ShapeDtypeStruct((64, 8, 128), BF),
        in_specs=[pl.BlockSpec(memory_space=pltpu.SMEM)] + [vmem] * 12,
        out_specs=vmem,
        scratch_shapes=[
            pltpu.VMEM((8, LANES), F32),
            pltpu.VMEM((2, 8, LANES), F32),
            pltpu.VMEM((64, LANES), BF),
            pltpu.VMEM((8, LANES), F32),
            pltpu.VMEM((128, LANES), BF),
            pltpu.VMEM((64, LANES), BF),
            pltpu.VMEM((64, LANES), BF),
            pltpu.VMEM((64, LANES), BF),
            pltpu.VMEM((64, LANES), BF),
            pltpu.VMEM((128, LANES), BF),
            pltpu.VMEM((384, LANES), F32),
            pltpu.VMEM((72, LANES), F32),
            pltpu.VMEM((288, LANES), F32),
        ],
        compiler_params=pltpu.CompilerParams(vmem_limit_bytes=48 << 20),
        cost_estimate=pl.CostEstimate(
            flops=2_000_000_000, bytes_accessed=4_000_000, transcendentals=0
        ),
        name="network",
    )(place, ext, above, below, *weights)


def rows_kernel(z_ref, o_ref):
    lane = iota((4, 128), 1)
    head = lane < 110

    def halves(source):
        turned = pltpu.roll(z_ref[source].astype(F32), 110, 1)
        return turned[:4], turned[4:]

    count = z_ref.shape[0]
    first, second = halves(0)
    opening = first
    for source in range(count):
        following = halves(source + 1) if source + 1 < count else (opening, None)
        at = 256 * source
        early = jnp.where(head, first, second)
        later = jnp.where(head, second, following[0])
        for plane in range(3):
            o_ref[plane, :, at : at + 128] = early[plane : plane + 1]
            o_ref[plane, :, at + 128 : at + 256] = later[plane : plane + 1]
        first, second = following


def run_rows(received):
    vmem = pl.BlockSpec(memory_space=pltpu.VMEM)
    return pl.pallas_call(
        rows_kernel,
        out_shape=jax.ShapeDtypeStruct((3, 1, 256 * received.shape[0]), F32),
        in_specs=[vmem],
        out_specs=vmem,
        compiler_params=pltpu.CompilerParams(vmem_limit_bytes=8 << 20),
        name="rows",
    )(received)


def on_device(decoded, loop_in, loop_out, first_conv, d1, d2, d3, d4, d5, head_conv):
    cols = lax.axis_size("col")
    rows = lax.axis_size("row")
    weights = run_prep(
        loop_in.transpose(0, 2, 1), loop_out, first_conv.transpose(0, 2, 1),
        d1, d2, d3, d4, d5, head_conv,
    )
    left = lax.ppermute(decoded, "col", [(i, (i + 1) % cols) for i in range(cols)])
    ext = jnp.stack([left, decoded])
    above = lax.ppermute(ext, "row", [(i, i + 1) for i in range(rows - 1)])
    below = lax.ppermute(ext, "row", [(i + 1, i) for i in range(rows - 1)])
    place = jnp.stack([lax.axis_index("row"), lax.axis_index("col")]).astype(jnp.int32)
    sent = run_main(place, ext, above, below, weights)
    received = lax.all_to_all(sent, "col", split_axis=0, concat_axis=0, tiled=True)
    return run_rows(received).transpose(1, 0, 2)[None]


def solution(mesh):
    in_specs = (P(None, "row", "col"), P(), P(), P(), P(), P(), P(), P(), P(), P())
    out_specs = P("row", "col", None, None)
    return jax.shard_map(
        on_device, mesh=mesh, in_specs=in_specs, out_specs=out_specs, check_vma=False
    )
```

```python
import jax
import jax.numpy as jnp
from jax import lax
from jax.experimental import pallas as pl
from jax.experimental.pallas import tpu as pltpu
from jax.sharding import PartitionSpec as P

BF = jnp.bfloat16
F32 = jnp.float32

STRIDE = 147
BASE = 128
PAIRS = 26
LANES = 4096
STEP = 1024
HALO = 9
SOURCE = ((1, -1), (0, 0), (1, 0), (0, 1))


def shift_of(pair, tap):
    return pair * STRIDE + tap - 1


def tiles_of(layer):
    first = (layer + 1) // 2
    last = (50 - layer) // 2
    low = (BASE + first * STRIDE) // 128 * 128
    high = -(-(BASE + (last + 1) * STRIDE) // 128) * 128
    return [(start, min(STEP, high - start)) for start in range(low, high, STEP)]


def iota(shape, dim):
    return lax.broadcasted_iota(jnp.int32, shape, dim)


def place_at(pair, phase):
    return 2 * pair + phase + 1


def picking(rows, depth, entries):
    return jnp.where(entries(iota((rows, depth), 0), iota((rows, depth), 1)), 1.0, 0.0).astype(BF)


def quotient(values, by):
    return lax.shift_right_arithmetic(values * (65536 // by + 1), 16)


def sections(pack):
    return (
        pack.at[896:960, 256:328],
        pack.at[896:976, 384:448],
        pack.at[896:1024, 128:200],
        pack.at[0:384, 0:768],
        pack.at[384:704, 0:384],
        pack.at[384:640, 384:768],
        pack.at[704:896, 0:384],
        pack.at[704:832, 384:768],
        pack.at[896:1184, 0:128],
    )


BANDS = ((896, 1184), (0, 384), (384, 704), (704, 896))


def band_copies(source, target, done):
    return [
        pltpu.make_async_copy(source.at[low:high, :], target.at[low:high, :], done.at[i])
        for i, (low, high) in enumerate(BANDS)
    ]


def prep_kernel(*refs):
    given, whole, held, pack, arrived, left = refs[:9], refs[9], refs[10:19], *refs[19:22]
    targets = sections(pack)
    leaving = band_copies(pack, whole, left)
    copies = [
        pltpu.make_async_copy(source, target, arrived.at[i])
        for i, (source, target) in enumerate(zip(given, held))
    ]
    for copy in copies:
        copy.start()
    for at in (0, 1, 2, 8):
        copies[at].wait()
    loop_in, loop_out, first_conv, d1, d2, d3, d4, d5, head = held
    w_in, w_out, w_first, w_f, w_1, w_2, w_3, w_4, w_head = targets
    for source, target in ((loop_in, w_in), (first_conv, w_first)):
        outs = source.shape[2]
        blank = jnp.zeros((1, outs), F32)
        flat = jnp.concatenate(
            [piece for t in range(9) for piece in (source[t].astype(F32), blank)], axis=0
        ).astype(BF)
        sides = []
        for p in range(2):

            def entries(m, k):
                group = lax.shift_right_arithmetic(m, 3)
                pair = quotient(group, 3)
                tap = group - 3 * pair
                down = 2 * pair - 1 + (lax.shift_right_arithmetic(m, 2) & 1) - p
                ok = (down >= 0) & (down <= 2) & ((m & 3) < 3)
                return ok & (k == (down * 3 + tap) * 4 + (m & 3))

            sides.append(jnp.dot(picking(72, 36, entries), flat, preferred_element_type=F32))
        target[...] = jnp.concatenate(sides, axis=1).T.astype(BF)
    blank = jnp.zeros((1, 32), F32)
    flat = jnp.concatenate(
        [piece for t in range(9) for piece in (loop_out[t].astype(F32), blank)], axis=0
    ).astype(BF)
    sides = []
    for q in range(2):

        def entries(m, k):
            group = lax.shift_right_arithmetic(m, 3)
            pair = quotient(group, 3)
            tap = group - 3 * pair
            down = 2 * pair - 1 + q - (lax.shift_right_arithmetic(m, 2) & 1)
            ok = (down >= 0) & (down <= 2) & ((m & 3) < 3)
            return ok & (k == (down * 3 + tap) * 4 + (m & 3))

        sides.append(jnp.dot(picking(80, 36, entries), flat, preferred_element_type=F32))
    w_out[...] = jnp.concatenate(sides, axis=1).astype(BF)
    blank = jnp.zeros((4, 64), F32)
    flat = jnp.concatenate(
        [piece for t in range(9) for piece in (head[t].astype(F32), blank)], axis=0
    ).astype(BF)
    sides = []
    for q in range(2):

        def entries(m, k):
            group = lax.shift_right_arithmetic(m, 5)
            pair = quotient(group, 3)
            tap = group - 3 * pair
            b = lax.shift_right_arithmetic(m, 4) & 1
            p = lax.shift_right_arithmetic(m, 3) & 1
            a = lax.shift_right_arithmetic(m, 2) & 1
            down = 2 * pair - 1 + q - p
            ok = (down >= 0) & (down <= 2) & ((m & 3) < 3)
            return ok & (k == (down * 3 + tap) * 16 + 4 * (m & 3) + 2 * a + b)

        sides.append(jnp.dot(picking(288, 144, entries), flat, preferred_element_type=F32))
    w_head[...] = jnp.concatenate(sides, axis=1).astype(BF)
    leaving[0].start()
    for at in range(3, 8):
        copies[at].wait()
    dense = (d1, d2, d3, d4, d5)
    for source, target in enumerate((w_f, w_1, w_2, w_3, w_4)):
        low = 0 if source == 0 else 32 + 32 * source
        ins = 64 if source == 0 else 32
        row = 0
        for weight in dense[source:]:
            outs = weight.shape[1]
            taps = [weight[t, :, low : low + ins] for t in range(9)]
            none = jnp.zeros((outs, 3 * ins), BF)
            joined = jnp.concatenate(taps, axis=1)
            target[row : row + outs, :] = jnp.concatenate([joined, none], axis=1)
            target[row + outs : row + 2 * outs, :] = jnp.concatenate([none, joined], axis=1)
            row += 2 * outs
        if source in (0, 2, 4):
            leaving[1 + source // 2].start()
    for copy in leaving:
        copy.wait()


def run_prep(*weights):
    return pl.pallas_call(
        prep_kernel,
        out_shape=jax.ShapeDtypeStruct((1184, 768), BF),
        in_specs=[pl.BlockSpec(memory_space=pltpu.HBM)] * 9,
        out_specs=pl.BlockSpec(memory_space=pltpu.HBM),
        scratch_shapes=[pltpu.VMEM(weight.shape, BF) for weight in weights]
        + [
            pltpu.VMEM((1184, 768), BF),
            pltpu.SemaphoreType.DMA((9,)),
            pltpu.SemaphoreType.DMA((4,)),
        ],
        compiler_params=pltpu.CompilerParams(vmem_limit_bytes=56 << 20),
        cost_estimate=pl.CostEstimate(flops=20_000_000, bytes_accessed=3_000_000, transcendentals=0),
        name="weights",
    )(*weights)


def lrelu(values):
    return jnp.maximum(values, 0.2 * values)


def main_kernel(
    place, ext, above, below, pack, y_ref,
    x0, mask, hid, fil, xf, x1, x2, x3, x4, xb, acc, zs, hs,
):
    w_in, w_out, w_first, w_f, w_1, w_2, w_3, w_4, w_head = sections(pack)
    row_at = place[0]
    col_at = place[1]
    for ref in (x0, hid, fil, xf, x1, x2, x3, x4, xb, zs):
        ref[...] = jnp.zeros(ref.shape, ref.dtype)

    lane = iota((8, LANES), 1) - BASE
    pair = lax.shift_right_arithmetic(lane * 28533, 22)
    column = lane - pair * STRIDE
    first_column = jnp.where(col_at == 0, 2 * HALO, 0)
    across = jnp.logical_and(column >= first_column, column < STRIDE - 1)
    for phase in range(2):
        row = 2 * pair + phase - 1 - HALO + 32 * row_at
        keep = jnp.logical_and(jnp.logical_and(row >= 0, row < 256), across)
        mask[phase] = jnp.where(keep, 1.0, 0.0)

    def masked(values, phase, start):
        rows, width = values.shape
        inside = mask[phase, :, start : start + width]
        return (values.reshape(rows // 8, 8, width) * inside[None]).reshape(rows, width)

    def wide(ref, plane):
        return jnp.concatenate([ref[0, plane], ref[1, plane]], axis=1)

    stacked = jnp.concatenate(
        [wide(ref, plane) for plane in range(3) for ref in (above, ext, below)], axis=0
    )
    rows = 8 * PAIRS
    m_at = iota((rows, 288), 0)
    k_at = iota((rows, 288), 1)
    stored = 2 * lax.shift_right_arithmetic(m_at, 3) + (lax.shift_right_arithmetic(m_at, 2) & 1)
    plane_at = m_at & 3
    pick = (plane_at < 3) & (stored >= 1) & (stored <= 50) & (k_at == plane_at * 96 + stored + 22)
    ordered = jnp.dot(
        jnp.where(pick, 1.0, 0.0).astype(BF), stacked, preferred_element_type=F32
    ).astype(BF)
    i_at = iota((256, 256), 0) - 110
    o_at = iota((256, 256), 1)
    place_cols = jnp.where(i_at == o_at, 1.0, 0.0).astype(BF)
    laid = jnp.dot(ordered, place_cols, preferred_element_type=F32)
    for g in range(PAIRS):
        x0[:, BASE + g * STRIDE : BASE + (g + 1) * STRIDE] = laid[8 * g : 8 * g + 8, :STRIDE]

    shifts = [(pair, tap) for pair in (-1, 0, 1) for tap in range(3)]

    def narrow_columns(ref, start, width):
        pieces = [
            ref[:, start + shift_of(pair, tap) : start + shift_of(pair, tap) + width]
            for pair, tap in shifts
        ]
        return jnp.concatenate(pieces, axis=0).astype(BF)

    for start, width in tiles_of(1):
        values = lrelu(jnp.dot(w_in[...], narrow_columns(x0, start, width), preferred_element_type=F32))
        for phase in range(2):
            part = slice(32 * phase, 32 * phase + 32)
            hid[part, start : start + width] = masked(values[part], phase, start).astype(BF)
    for start, width in tiles_of(1):
        zs[:, start : start + width] = jnp.dot(
            w_out[...], hid[:, start : start + width], preferred_element_type=F32
        )
    for start, width in tiles_of(2):
        values = x0[:, start : start + width]
        for at, (pair_, tap) in enumerate(shifts):
            off = start + shift_of(pair_, tap)
            values = values + zs[8 * at : 8 * at + 8, off : off + width]
        inside = jnp.where(
            iota((8, width), 0) < 4, mask[0, :, start : start + width], mask[1, :, start : start + width]
        )
        fil[:, start : start + width] = (values * inside).astype(BF).astype(F32)

    for start, width in tiles_of(3):
        values = jnp.dot(w_first[...], narrow_columns(fil, start, width), preferred_element_type=F32)
        for phase in range(2):
            part = slice(64 * phase, 64 * phase + 64)
            xf[part, start : start + width] = masked(values[part], phase, start).astype(BF)

    def columns(ref, start, width):
        count = ref.shape[0] // 2
        pieces = []
        for phase, pair_ in SOURCE:
            for tap in range(3):
                off = start + shift_of(pair_, tap)
                pieces.append(ref[count * phase : count * (phase + 1), off : off + width])
        return jnp.concatenate(pieces, axis=0)

    for layer, (ref, weight, target) in enumerate(
        ((xf, w_f, x1), (x1, w_1, x2), (x2, w_2, x3), (x3, w_3, x4), (x4, w_4, xb))
    ):
        low = 64 * layer
        for start, width in tiles_of(4 + layer):
            span = slice(start, start + width)
            values = jnp.dot(weight[...], columns(ref, start, width), preferred_element_type=F32)
            if layer > 0:
                values = values + acc[low:, span]
            if layer < 4:
                acc[low + 64 :, span] = values[64:]
                values = lrelu(values[:64])
                count = 32
            else:
                values = xf[:, span].astype(F32) + 0.2 * values
                count = 64
            for phase in range(2):
                part = slice(count * phase, count * (phase + 1))
                target[part, span] = masked(values[part], phase, start).astype(BF)

    for start, width in tiles_of(8):
        hs[:, start : start + width] = jnp.dot(
            w_head[...], xb[:, start : start + width], preferred_element_type=F32
        )
    rows_out = []
    for g in range(5, 21):
        low = BASE + g * STRIDE
        values = None
        for at, (pair_, tap) in enumerate(shifts):
            off = low + shift_of(pair_, tap)
            term = hs[32 * at : 32 * at + 32, off : off + 256]
            values = term if values is None else values + term
        rows_out.append(values.astype(BF))
    even = jnp.concatenate([values[:16] for values in rows_out], axis=0)
    odd = jnp.concatenate([values[16:] for values in rows_out], axis=0)
    k_at = iota((256, 384), 0)
    n_at = iota((256, 384), 1)
    over = n_at - 256
    turn = jnp.where(over >= 36, over - 36, jnp.where(over >= 18, over - 18, over))
    wanted = jnp.where(over < 0, n_at, 256 + turn)
    cell = lax.shift_right_arithmetic(wanted, 1) + HALO
    spread = [
        jnp.where((k_at == cell) & ((wanted & 1) == b), 1.0, 0.0).astype(BF) for b in range(2)
    ]
    result = jnp.dot(even, spread[0], preferred_element_type=F32) + jnp.dot(
        odd, spread[1], preferred_element_type=F32
    )
    first = result[:, :128].reshape(32, 8, 128)
    second = result[:, 128:256].reshape(32, 8, 128)
    sub8 = iota((32, 8, 128), 1)
    lane8 = iota((32, 8, 128), 2)
    low8 = 18 * (sub8 & 3)
    extra = jnp.where(
        (lane8 >= low8) & (lane8 < low8 + 18), result[:, 256:].reshape(32, 8, 128), 0.0
    )
    extra = extra + pltpu.roll(extra, 1, 1) + pltpu.roll(extra, 2, 1)
    first = jnp.where((sub8 & 3) == 3, pltpu.roll(extra, 1, 1), first)
    top = sub8 < 4
    even_rows = jnp.where(top, first, pltpu.roll(second, 4, 1)).astype(BF)
    odd_rows = jnp.where(top, pltpu.roll(first, 4, 1), second).astype(BF)
    for i in range(32):
        y_ref[2 * i] = even_rows[i]
        y_ref[2 * i + 1] = odd_rows[i]


def run_main(place, ext, above, below, pack):
    vmem = pl.BlockSpec(memory_space=pltpu.VMEM)
    return pl.pallas_call(
        main_kernel,
        out_shape=jax.ShapeDtypeStruct((64, 8, 128), BF),
        in_specs=[pl.BlockSpec(memory_space=pltpu.SMEM)] + [vmem] * 4,
        out_specs=vmem,
        scratch_shapes=[
            pltpu.VMEM((8, LANES), F32),
            pltpu.VMEM((2, 8, LANES), F32),
            pltpu.VMEM((64, LANES), BF),
            pltpu.VMEM((8, LANES), F32),
            pltpu.VMEM((128, LANES), BF),
            pltpu.VMEM((64, LANES), BF),
            pltpu.VMEM((64, LANES), BF),
            pltpu.VMEM((64, LANES), BF),
            pltpu.VMEM((64, LANES), BF),
            pltpu.VMEM((128, LANES), BF),
            pltpu.VMEM((384, LANES), F32),
            pltpu.VMEM((80, LANES), F32),
            pltpu.VMEM((288, LANES), F32),
        ],
        compiler_params=pltpu.CompilerParams(vmem_limit_bytes=44 << 20),
        cost_estimate=pl.CostEstimate(
            flops=2_000_000_000, bytes_accessed=4_000_000, transcendentals=0
        ),
        name="network",
    )(place, ext, above, below, pack)


def rows_kernel(z_ref, o_ref):
    lane = iota((4, 128), 1)
    head = lane < 110

    def halves(source):
        turned = pltpu.roll(z_ref[source].astype(F32), 110, 1)
        return turned[:4], turned[4:]

    count = z_ref.shape[0]
    first, second = halves(0)
    spare = z_ref[count - 1].astype(F32)[3:4]
    closing = jnp.concatenate(
        [pltpu.roll(spare, 110 - 18 * plane, 1) for plane in range(3)] + [spare], axis=0
    )
    for source in range(count):
        following = halves(source + 1) if source + 1 < count else (closing, None)
        at = 256 * source
        early = jnp.where(head, first, second)
        later = jnp.where(head, second, following[0])
        for plane in range(3):
            o_ref[plane, :, at : at + 128] = early[plane : plane + 1]
            o_ref[plane, :, at + 128 : at + 256] = later[plane : plane + 1]
        first, second = following


def run_rows(received):
    vmem = pl.BlockSpec(memory_space=pltpu.VMEM)
    return pl.pallas_call(
        rows_kernel,
        out_shape=jax.ShapeDtypeStruct((3, 1, 256 * received.shape[0]), F32),
        in_specs=[vmem],
        out_specs=vmem,
        compiler_params=pltpu.CompilerParams(vmem_limit_bytes=8 << 20),
        name="rows",
    )(received)


def on_device(decoded, loop_in, loop_out, first_conv, d1, d2, d3, d4, d5, head_conv):
    cols = lax.axis_size("col")
    rows = lax.axis_size("row")
    pack = run_prep(
        loop_in.transpose(0, 2, 1), loop_out, first_conv.transpose(0, 2, 1),
        d1, d2, d3, d4, d5, head_conv,
    )
    left = lax.ppermute(decoded, "col", [(i, i + 1) for i in range(cols - 1)])
    ext = jnp.stack([left, decoded])
    above = lax.ppermute(ext, "row", [(i, i + 1) for i in range(rows - 1)])
    below = lax.ppermute(ext, "row", [(i + 1, i) for i in range(rows - 1)])
    place = jnp.stack([lax.axis_index("row"), lax.axis_index("col")]).astype(jnp.int32)
    sent = run_main(place, ext, above, below, pack)
    received = lax.all_to_all(sent, "col", split_axis=0, concat_axis=0, tiled=True)
    return run_rows(received).transpose(1, 0, 2)[None]


def solution(mesh):
    in_specs = (P(None, "row", "col"), P(), P(), P(), P(), P(), P(), P(), P(), P())
    out_specs = P("row", "col", None, None)
    return jax.shard_map(
        on_device, mesh=mesh, in_specs=in_specs, out_specs=out_specs, check_vma=False
    )
```

```python
import jax
import jax.numpy as jnp
from jax import lax
from jax.experimental import pallas as pl
from jax.experimental.pallas import tpu as pltpu
from jax.sharding import PartitionSpec as P

BF = jnp.bfloat16
F32 = jnp.float32

STRIDE = 147
BASE = 128
PAIRS = 26
END = BASE + PAIRS * STRIDE
LANES = 4096
STEP = 1024
HALO = 9
SOURCE = ((1, -1), (0, 0), (1, 0), (0, 1))


def shift_of(pair, tap):
    return pair * STRIDE + tap - 1


def tiles_of(layer):
    first = (layer + 1) // 2
    last = (50 - layer) // 2
    low = (BASE + first * STRIDE) // 128 * 128
    high = -(-(BASE + (last + 1) * STRIDE) // 128) * 128
    return [(start, min(STEP, high - start)) for start in range(low, high, STEP)]


def iota(shape, dim):
    return lax.broadcasted_iota(jnp.int32, shape, dim)


def place_at(pair, phase):
    return 2 * pair + phase + 1


def picking(rows, depth, entries):
    return jnp.where(entries(iota((rows, depth), 0), iota((rows, depth), 1)), 1.0, 0.0).astype(BF)


def quotient(values, by):
    return lax.shift_right_arithmetic(values * (65536 // by + 1), 16)


def sections(pack):
    return (
        pack.at[896:960, 256:328],
        pack.at[896:976, 384:448],
        pack.at[896:1024, 128:200],
        pack.at[0:384, 0:768],
        pack.at[384:704, 0:384],
        pack.at[384:640, 384:768],
        pack.at[704:896, 0:384],
        pack.at[704:832, 384:768],
        pack.at[896:1184, 0:128],
    )


BANDS = ((896, 1184), (0, 384), (384, 704), (704, 896))


def band_copies(source, target, done):
    return [
        pltpu.make_async_copy(source.at[low:high, :], target.at[low:high, :], done.at[i])
        for i, (low, high) in enumerate(BANDS)
    ]


def prep_kernel(*refs):
    given, whole, held, pack, arrived, left = refs[:9], refs[9], refs[10:19], *refs[19:22]
    targets = sections(pack)
    leaving = band_copies(pack, whole, left)
    copies = [
        pltpu.make_async_copy(source, target, arrived.at[i])
        for i, (source, target) in enumerate(zip(given, held))
    ]
    for copy in copies:
        copy.start()
    for at in (0, 1, 2, 8):
        copies[at].wait()
    loop_in, loop_out, first_conv, d1, d2, d3, d4, d5, head = held
    w_in, w_out, w_first, w_f, w_1, w_2, w_3, w_4, w_head = targets
    for source, target in ((loop_in, w_in), (first_conv, w_first)):
        outs = source.shape[2]
        blank = jnp.zeros((1, outs), F32)
        flat = jnp.concatenate(
            [piece for t in range(9) for piece in (source[t].astype(F32), blank)], axis=0
        ).astype(BF)
        sides = []
        for p in range(2):

            def entries(m, k):
                group = lax.shift_right_arithmetic(m, 3)
                pair = quotient(group, 3)
                tap = group - 3 * pair
                down = 2 * pair - 1 + (lax.shift_right_arithmetic(m, 2) & 1) - p
                ok = (down >= 0) & (down <= 2) & ((m & 3) < 3)
                return ok & (k == (down * 3 + tap) * 4 + (m & 3))

            sides.append(jnp.dot(picking(72, 36, entries), flat, preferred_element_type=F32))
        target[...] = jnp.concatenate(sides, axis=1).T.astype(BF)
    blank = jnp.zeros((1, 32), F32)
    flat = jnp.concatenate(
        [piece for t in range(9) for piece in (loop_out[t].astype(F32), blank)], axis=0
    ).astype(BF)
    sides = []
    for q in range(2):

        def entries(m, k):
            group = lax.shift_right_arithmetic(m, 3)
            pair = quotient(group, 3)
            tap = group - 3 * pair
            down = 2 * pair - 1 + q - (lax.shift_right_arithmetic(m, 2) & 1)
            ok = (down >= 0) & (down <= 2) & ((m & 3) < 3)
            return ok & (k == (down * 3 + tap) * 4 + (m & 3))

        sides.append(jnp.dot(picking(80, 36, entries), flat, preferred_element_type=F32))
    w_out[...] = jnp.concatenate(sides, axis=1).astype(BF)
    blank = jnp.zeros((4, 64), F32)
    flat = jnp.concatenate(
        [piece for t in range(9) for piece in (head[t].astype(F32), blank)], axis=0
    ).astype(BF)
    sides = []
    for q in range(2):

        def entries(m, k):
            group = lax.shift_right_arithmetic(m, 5)
            pair = quotient(group, 3)
            tap = group - 3 * pair
            b = lax.shift_right_arithmetic(m, 4) & 1
            p = lax.shift_right_arithmetic(m, 3) & 1
            a = lax.shift_right_arithmetic(m, 2) & 1
            down = 2 * pair - 1 + q - p
            ok = (down >= 0) & (down <= 2) & ((m & 3) < 3)
            return ok & (k == (down * 3 + tap) * 16 + 4 * (m & 3) + 2 * a + b)

        sides.append(jnp.dot(picking(288, 144, entries), flat, preferred_element_type=F32))
    w_head[...] = jnp.concatenate(sides, axis=1).astype(BF)
    leaving[0].start()
    for at in range(3, 8):
        copies[at].wait()
    dense = (d1, d2, d3, d4, d5)
    for source, target in enumerate((w_f, w_1, w_2, w_3, w_4)):
        low = 0 if source == 0 else 32 + 32 * source
        ins = 64 if source == 0 else 32
        row = 0
        for weight in dense[source:]:
            outs = weight.shape[1]
            taps = [weight[t, :, low : low + ins] for t in range(9)]
            none = jnp.zeros((outs, 3 * ins), BF)
            joined = jnp.concatenate(taps, axis=1)
            target[row : row + outs, :] = jnp.concatenate([joined, none], axis=1)
            target[row + outs : row + 2 * outs, :] = jnp.concatenate([none, joined], axis=1)
            row += 2 * outs
        if source in (0, 2, 4):
            leaving[1 + source // 2].start()
    for copy in leaving:
        copy.wait()


def run_prep(*weights):
    return pl.pallas_call(
        prep_kernel,
        out_shape=jax.ShapeDtypeStruct((1184, 768), BF),
        in_specs=[pl.BlockSpec(memory_space=pltpu.HBM)] * 9,
        out_specs=pl.BlockSpec(memory_space=pltpu.HBM),
        scratch_shapes=[pltpu.VMEM(weight.shape, BF) for weight in weights]
        + [
            pltpu.VMEM((1184, 768), BF),
            pltpu.SemaphoreType.DMA((9,)),
            pltpu.SemaphoreType.DMA((4,)),
        ],
        compiler_params=pltpu.CompilerParams(vmem_limit_bytes=56 << 20),
        cost_estimate=pl.CostEstimate(flops=20_000_000, bytes_accessed=3_000_000, transcendentals=0),
        name="weights",
    )(*weights)


def lrelu(values):
    return jnp.maximum(values, 0.2 * values)


def main_kernel(
    place, ext, above, below, pack, y_ref,
    x0, mask, hid, fil, xf, x1, x2, x3, x4, xb, acc, zs, hs,
):
    w_in, w_out, w_first, w_f, w_1, w_2, w_3, w_4, w_head = sections(pack)
    row_at = place[0]
    col_at = place[1]
    x0[:, :BASE] = jnp.zeros((8, BASE), F32)
    x0[:, END:] = jnp.zeros((8, LANES - END), F32)
    for layer, written in (
        (1, (zs,)), (2, (fil,)), (3, (xf,)), (4, (x1,)), (5, (x2,)), (6, (x3,)), (7, (x4,)), (8, (hs,))
    ):
        spans = tiles_of(layer)
        low, high = spans[0][0], spans[-1][0] + spans[-1][1]
        for ref in written:
            for side in (slice(max(low - 256, 0), low), slice(high, min(high + 256, LANES))):
                ref[:, side] = jnp.zeros((ref.shape[0], side.stop - side.start), ref.dtype)

    lane = iota((8, LANES), 1) - BASE
    pair = lax.shift_right_arithmetic(lane * 28533, 22)
    column = lane - pair * STRIDE
    first_column = jnp.where(col_at == 0, 2 * HALO, 0)
    across = jnp.logical_and(column >= first_column, column < STRIDE - 1)
    for phase in range(2):
        row = 2 * pair + phase - 1 - HALO + 32 * row_at
        keep = jnp.logical_and(jnp.logical_and(row >= 0, row < 256), across)
        mask[phase] = jnp.where(keep, 1.0, 0.0)

    def masked(values, phase, start):
        rows, width = values.shape
        inside = mask[phase, :, start : start + width]
        return (values.reshape(rows // 8, 8, width) * inside[None]).reshape(rows, width)

    def wide(ref, plane):
        return jnp.concatenate([ref[0, plane], ref[1, plane]], axis=1)

    stacked = jnp.concatenate(
        [wide(ref, plane) for plane in range(3) for ref in (above, ext, below)], axis=0
    )
    rows = 8 * PAIRS
    m_at = iota((rows, 288), 0)
    k_at = iota((rows, 288), 1)
    stored = 2 * lax.shift_right_arithmetic(m_at, 3) + (lax.shift_right_arithmetic(m_at, 2) & 1)
    plane_at = m_at & 3
    pick = (plane_at < 3) & (stored >= 1) & (stored <= 50) & (k_at == plane_at * 96 + stored + 22)
    ordered = jnp.dot(
        jnp.where(pick, 1.0, 0.0).astype(BF), stacked, preferred_element_type=F32
    ).astype(BF)
    i_at = iota((256, 256), 0) - 110
    o_at = iota((256, 256), 1)
    place_cols = jnp.where(i_at == o_at, 1.0, 0.0).astype(BF)
    laid = jnp.dot(ordered, place_cols, preferred_element_type=F32)
    for g in range(PAIRS):
        x0[:, BASE + g * STRIDE : BASE + (g + 1) * STRIDE] = laid[8 * g : 8 * g + 8, :STRIDE]

    shifts = [(pair, tap) for pair in (-1, 0, 1) for tap in range(3)]

    def narrow_columns(ref, start, width):
        pieces = [
            ref[:, start + shift_of(pair, tap) : start + shift_of(pair, tap) + width]
            for pair, tap in shifts
        ]
        return jnp.concatenate(pieces, axis=0).astype(BF)

    for start, width in tiles_of(1):
        values = lrelu(jnp.dot(w_in[...], narrow_columns(x0, start, width), preferred_element_type=F32))
        for phase in range(2):
            part = slice(32 * phase, 32 * phase + 32)
            hid[part, start : start + width] = masked(values[part], phase, start).astype(BF)
    for start, width in tiles_of(1):
        zs[:, start : start + width] = jnp.dot(
            w_out[...], hid[:, start : start + width], preferred_element_type=F32
        )
    for start, width in tiles_of(2):
        values = x0[:, start : start + width]
        for at, (pair_, tap) in enumerate(shifts):
            off = start + shift_of(pair_, tap)
            values = values + zs[8 * at : 8 * at + 8, off : off + width]
        inside = jnp.where(
            iota((8, width), 0) < 4, mask[0, :, start : start + width], mask[1, :, start : start + width]
        )
        fil[:, start : start + width] = (values * inside).astype(BF).astype(F32)

    for start, width in tiles_of(3):
        values = jnp.dot(w_first[...], narrow_columns(fil, start, width), preferred_element_type=F32)
        for phase in range(2):
            part = slice(64 * phase, 64 * phase + 64)
            xf[part, start : start + width] = masked(values[part], phase, start).astype(BF)

    def columns(ref, start, width):
        count = ref.shape[0] // 2
        pieces = []
        for phase, pair_ in SOURCE:
            for tap in range(3):
                off = start + shift_of(pair_, tap)
                pieces.append(ref[count * phase : count * (phase + 1), off : off + width])
        return jnp.concatenate(pieces, axis=0)

    for layer, (ref, weight, target) in enumerate(
        ((xf, w_f, x1), (x1, w_1, x2), (x2, w_2, x3), (x3, w_3, x4), (x4, w_4, xb))
    ):
        low = 64 * layer
        for start, width in tiles_of(4 + layer):
            span = slice(start, start + width)
            values = jnp.dot(weight[...], columns(ref, start, width), preferred_element_type=F32)
            if layer > 0:
                values = values + acc[low:, span]
            if layer < 4:
                acc[low + 64 :, span] = values[64:]
                values = lrelu(values[:64])
                count = 32
            else:
                values = xf[:, span].astype(F32) + 0.2 * values
                count = 64
            for phase in range(2):
                part = slice(count * phase, count * (phase + 1))
                target[part, span] = masked(values[part], phase, start).astype(BF)

    for start, width in tiles_of(8):
        hs[:, start : start + width] = jnp.dot(
            w_head[...], xb[:, start : start + width], preferred_element_type=F32
        )
    rows_out = []
    for g in range(5, 21):
        low = BASE + g * STRIDE
        values = None
        for at, (pair_, tap) in enumerate(shifts):
            off = low + shift_of(pair_, tap)
            term = hs[32 * at : 32 * at + 32, off : off + 256]
            values = term if values is None else values + term
        rows_out.append(values.astype(BF))
    even = jnp.concatenate([values[:16] for values in rows_out], axis=0)
    odd = jnp.concatenate([values[16:] for values in rows_out], axis=0)
    k_at = iota((256, 384), 0)
    n_at = iota((256, 384), 1)
    over = n_at - 256
    turn = jnp.where(over >= 36, over - 36, jnp.where(over >= 18, over - 18, over))
    wanted = jnp.where(over < 0, n_at, 256 + turn)
    cell = lax.shift_right_arithmetic(wanted, 1) + HALO
    spread = [
        jnp.where((k_at == cell) & ((wanted & 1) == b), 1.0, 0.0).astype(BF) for b in range(2)
    ]
    result = jnp.dot(even, spread[0], preferred_element_type=F32) + jnp.dot(
        odd, spread[1], preferred_element_type=F32
    )
    first = result[:, :128].reshape(32, 8, 128)
    second = result[:, 128:256].reshape(32, 8, 128)
    sub8 = iota((32, 8, 128), 1)
    lane8 = iota((32, 8, 128), 2)
    low8 = 18 * (sub8 & 3)
    extra = jnp.where(
        (lane8 >= low8) & (lane8 < low8 + 18), result[:, 256:].reshape(32, 8, 128), 0.0
    )
    extra = extra + pltpu.roll(extra, 1, 1) + pltpu.roll(extra, 2, 1)
    first = jnp.where((sub8 & 3) == 3, pltpu.roll(extra, 1, 1), first)
    top = sub8 < 4
    even_rows = jnp.where(top, first, pltpu.roll(second, 4, 1)).astype(BF)
    odd_rows = jnp.where(top, pltpu.roll(first, 4, 1), second).astype(BF)
    for i in range(32):
        y_ref[2 * i] = even_rows[i]
        y_ref[2 * i + 1] = odd_rows[i]


def run_main(place, ext, above, below, pack):
    vmem = pl.BlockSpec(memory_space=pltpu.VMEM)
    return pl.pallas_call(
        main_kernel,
        out_shape=jax.ShapeDtypeStruct((64, 8, 128), BF),
        in_specs=[pl.BlockSpec(memory_space=pltpu.SMEM)] + [vmem] * 4,
        out_specs=vmem,
        scratch_shapes=[
            pltpu.VMEM((8, LANES), F32),
            pltpu.VMEM((2, 8, LANES), F32),
            pltpu.VMEM((64, LANES), BF),
            pltpu.VMEM((8, LANES), F32),
            pltpu.VMEM((128, LANES), BF),
            pltpu.VMEM((64, LANES), BF),
            pltpu.VMEM((64, LANES), BF),
            pltpu.VMEM((64, LANES), BF),
            pltpu.VMEM((64, LANES), BF),
            pltpu.VMEM((128, LANES), BF),
            pltpu.VMEM((384, LANES), F32),
            pltpu.VMEM((80, LANES), F32),
            pltpu.VMEM((288, LANES), F32),
        ],
        compiler_params=pltpu.CompilerParams(vmem_limit_bytes=44 << 20),
        cost_estimate=pl.CostEstimate(
            flops=2_000_000_000, bytes_accessed=4_000_000, transcendentals=0
        ),
        name="network",
    )(place, ext, above, below, pack)


def rows_kernel(z_ref, o_ref):
    lane = iota((4, 128), 1)
    head = lane < 110

    def halves(source):
        turned = pltpu.roll(z_ref[source].astype(F32), 110, 1)
        return turned[:4], turned[4:]

    count = z_ref.shape[0]
    first, second = halves(0)
    spare = z_ref[count - 1].astype(F32)[3:4]
    closing = jnp.concatenate(
        [pltpu.roll(spare, 110 - 18 * plane, 1) for plane in range(3)] + [spare], axis=0
    )
    for source in range(count):
        following = halves(source + 1) if source + 1 < count else (closing, None)
        at = 256 * source
        early = jnp.where(head, first, second)
        later = jnp.where(head, second, following[0])
        for plane in range(3):
            o_ref[plane, :, at : at + 128] = early[plane : plane + 1]
            o_ref[plane, :, at + 128 : at + 256] = later[plane : plane + 1]
        first, second = following


def run_rows(received):
    vmem = pl.BlockSpec(memory_space=pltpu.VMEM)
    return pl.pallas_call(
        rows_kernel,
        out_shape=jax.ShapeDtypeStruct((3, 1, 256 * received.shape[0]), F32),
        in_specs=[vmem],
        out_specs=vmem,
        compiler_params=pltpu.CompilerParams(vmem_limit_bytes=8 << 20),
        name="rows",
    )(received)


def on_device(decoded, loop_in, loop_out, first_conv, d1, d2, d3, d4, d5, head_conv):
    cols = lax.axis_size("col")
    rows = lax.axis_size("row")
    pack = run_prep(
        loop_in.transpose(0, 2, 1), loop_out, first_conv.transpose(0, 2, 1),
        d1, d2, d3, d4, d5, head_conv,
    )
    left = lax.ppermute(decoded, "col", [(i, i + 1) for i in range(cols - 1)])
    left, pack = lax.optimization_barrier((left, pack))
    ext = jnp.stack([left, decoded])
    above = lax.ppermute(ext, "row", [(i, i + 1) for i in range(rows - 1)])
    below = lax.ppermute(ext, "row", [(i + 1, i) for i in range(rows - 1)])
    place = jnp.stack([lax.axis_index("row"), lax.axis_index("col")]).astype(jnp.int32)
    sent = run_main(place, ext, above, below, pack)
    received = lax.all_to_all(sent, "col", split_axis=0, concat_axis=0, tiled=True)
    return run_rows(received).transpose(1, 0, 2)[None]


def solution(mesh):
    in_specs = (P(None, "row", "col"), P(), P(), P(), P(), P(), P(), P(), P(), P())
    out_specs = P("row", "col", None, None)
    return jax.shard_map(
        on_device, mesh=mesh, in_specs=in_specs, out_specs=out_specs, check_vma=False
    )
```

```python
import jax
import jax.numpy as jnp
from jax import lax
from jax.experimental import pallas as pl
from jax.experimental.pallas import tpu as pltpu
from jax.sharding import PartitionSpec as P

BF = jnp.bfloat16
F32 = jnp.float32

STRIDE = 147
BASE = 128
PAIRS = 26
END = BASE + PAIRS * STRIDE
LANES = 4096
STEP = 1024
HALO = 9
SOURCE = ((1, -1), (0, 0), (1, 0), (0, 1))


def shift_of(pair, tap):
    return pair * STRIDE + tap - 1


def tiles_of(layer):
    first = (layer + 1) // 2
    last = (50 - layer) // 2
    low = (BASE + first * STRIDE) // 128 * 128
    high = -(-(BASE + (last + 1) * STRIDE) // 128) * 128
    return [(start, min(STEP, high - start)) for start in range(low, high, STEP)]


def iota(shape, dim):
    return lax.broadcasted_iota(jnp.int32, shape, dim)


def place_at(pair, phase):
    return 2 * pair + phase + 1


def picking(rows, depth, entries):
    return jnp.where(entries(iota((rows, depth), 0), iota((rows, depth), 1)), 1.0, 0.0).astype(BF)


def quotient(values, by):
    return lax.shift_right_arithmetic(values * (65536 // by + 1), 16)


def sections(pack):
    return (
        pack.at[896:960, 256:328],
        pack.at[896:976, 384:448],
        pack.at[896:1024, 128:200],
        pack.at[0:384, 0:768],
        pack.at[384:704, 0:384],
        pack.at[384:640, 384:768],
        pack.at[704:896, 0:384],
        pack.at[704:832, 384:768],
        pack.at[896:1184, 0:128],
    )


BANDS = ((896, 1184), (0, 384), (384, 704), (704, 896))


def band_copies(source, target, done):
    return [
        pltpu.make_async_copy(source.at[low:high, :], target.at[low:high, :], done.at[i])
        for i, (low, high) in enumerate(BANDS)
    ]


def prep_kernel(*refs):
    given, whole, held, pack, arrived, left = refs[:9], refs[9], refs[10:19], *refs[19:22]
    targets = sections(pack)
    leaving = band_copies(pack, whole, left)
    copies = [
        pltpu.make_async_copy(source, target, arrived.at[i])
        for i, (source, target) in enumerate(zip(given, held))
    ]
    for copy in copies:
        copy.start()
    for at in (0, 1, 2, 8):
        copies[at].wait()
    loop_in, loop_out, first_conv, d1, d2, d3, d4, d5, head = held
    w_in, w_out, w_first, w_f, w_1, w_2, w_3, w_4, w_head = targets
    for source, target in ((loop_in, w_in), (first_conv, w_first)):
        outs = source.shape[2]
        blank = jnp.zeros((1, outs), F32)
        flat = jnp.concatenate(
            [piece for t in range(9) for piece in (source[t].astype(F32), blank)], axis=0
        ).astype(BF)
        sides = []
        for p in range(2):

            def entries(m, k):
                group = lax.shift_right_arithmetic(m, 3)
                pair = quotient(group, 3)
                tap = group - 3 * pair
                down = 2 * pair - 1 + (lax.shift_right_arithmetic(m, 2) & 1) - p
                ok = (down >= 0) & (down <= 2) & ((m & 3) < 3)
                return ok & (k == (down * 3 + tap) * 4 + (m & 3))

            sides.append(jnp.dot(picking(72, 36, entries), flat, preferred_element_type=F32))
        target[...] = jnp.concatenate(sides, axis=1).T.astype(BF)
    blank = jnp.zeros((1, 32), F32)
    flat = jnp.concatenate(
        [piece for t in range(9) for piece in (loop_out[t].astype(F32), blank)], axis=0
    ).astype(BF)
    sides = []
    for q in range(2):

        def entries(m, k):
            group = lax.shift_right_arithmetic(m, 3)
            pair = quotient(group, 3)
            tap = group - 3 * pair
            down = 2 * pair - 1 + q - (lax.shift_right_arithmetic(m, 2) & 1)
            ok = (down >= 0) & (down <= 2) & ((m & 3) < 3)
            return ok & (k == (down * 3 + tap) * 4 + (m & 3))

        sides.append(jnp.dot(picking(80, 36, entries), flat, preferred_element_type=F32))
    w_out[...] = jnp.concatenate(sides, axis=1).astype(BF)
    blank = jnp.zeros((4, 64), F32)
    flat = jnp.concatenate(
        [piece for t in range(9) for piece in (head[t].astype(F32), blank)], axis=0
    ).astype(BF)
    sides = []
    for q in range(2):

        def entries(m, k):
            group = lax.shift_right_arithmetic(m, 5)
            pair = quotient(group, 3)
            tap = group - 3 * pair
            b = lax.shift_right_arithmetic(m, 4) & 1
            p = lax.shift_right_arithmetic(m, 3) & 1
            a = lax.shift_right_arithmetic(m, 2) & 1
            down = 2 * pair - 1 + q - p
            ok = (down >= 0) & (down <= 2) & ((m & 3) < 3)
            return ok & (k == (down * 3 + tap) * 16 + 4 * (m & 3) + 2 * a + b)

        sides.append(jnp.dot(picking(288, 144, entries), flat, preferred_element_type=F32))
    w_head[...] = jnp.concatenate(sides, axis=1).astype(BF)
    leaving[0].start()
    for at in range(3, 8):
        copies[at].wait()
    dense = (d1, d2, d3, d4, d5)
    for source, target in enumerate((w_f, w_1, w_2, w_3, w_4)):
        low = 0 if source == 0 else 32 + 32 * source
        ins = 64 if source == 0 else 32
        row = 0
        for weight in dense[source:]:
            outs = weight.shape[1]
            taps = [weight[t, :, low : low + ins] for t in range(9)]
            none = jnp.zeros((outs, 3 * ins), BF)
            joined = jnp.concatenate(taps, axis=1)
            target[row : row + outs, :] = jnp.concatenate([joined, none], axis=1)
            target[row + outs : row + 2 * outs, :] = jnp.concatenate([none, joined], axis=1)
            row += 2 * outs
        if source in (0, 2, 4):
            leaving[1 + source // 2].start()
    for copy in leaving:
        copy.wait()


def run_prep(*weights):
    return pl.pallas_call(
        prep_kernel,
        out_shape=jax.ShapeDtypeStruct((1184, 768), BF),
        in_specs=[pl.BlockSpec(memory_space=pltpu.HBM)] * 9,
        out_specs=pl.BlockSpec(memory_space=pltpu.HBM),
        scratch_shapes=[pltpu.VMEM(weight.shape, BF) for weight in weights]
        + [
            pltpu.VMEM((1184, 768), BF),
            pltpu.SemaphoreType.DMA((9,)),
            pltpu.SemaphoreType.DMA((4,)),
        ],
        compiler_params=pltpu.CompilerParams(vmem_limit_bytes=56 << 20),
        cost_estimate=pl.CostEstimate(flops=20_000_000, bytes_accessed=3_000_000, transcendentals=0),
        name="weights",
    )(*weights)


def lrelu(values):
    return jnp.maximum(values, 0.2 * values)


def main_kernel(
    place, left, own, above, below, pack, y_ref,
    x0, mask, hid, fil, xf, x1, x2, x3, x4, xb, acc, zs, hs,
):
    w_in, w_out, w_first, w_f, w_1, w_2, w_3, w_4, w_head = sections(pack)
    row_at = place[0]
    col_at = place[1]
    x0[:, :BASE] = jnp.zeros((8, BASE), F32)
    x0[:, END:] = jnp.zeros((8, LANES - END), F32)
    for layer, written in (
        (1, (zs,)), (2, (fil,)), (3, (xf,)), (4, (x1,)), (5, (x2,)), (6, (x3,)), (7, (x4,)), (8, (hs,))
    ):
        spans = tiles_of(layer)
        low, high = spans[0][0], spans[-1][0] + spans[-1][1]
        for ref in written:
            for side in (slice(max(low - 256, 0), low), slice(high, min(high + 256, LANES))):
                ref[:, side] = jnp.zeros((ref.shape[0], side.stop - side.start), ref.dtype)

    lane = iota((8, LANES), 1) - BASE
    pair = lax.shift_right_arithmetic(lane * 28533, 22)
    column = lane - pair * STRIDE
    first_column = jnp.where(col_at == 0, 2 * HALO, 0)
    across = jnp.logical_and(column >= first_column, column < STRIDE - 1)
    for phase in range(2):
        row = 2 * pair + phase - 1 - HALO + 32 * row_at
        keep = jnp.logical_and(jnp.logical_and(row >= 0, row < 256), across)
        mask[phase] = jnp.where(keep, 1.0, 0.0)

    def masked(values, phase, start):
        rows, width = values.shape
        inside = mask[phase, :, start : start + width]
        return (values.reshape(rows // 8, 8, width) * inside[None]).reshape(rows, width)

    stacked = jnp.concatenate(
        [
            piece
            for plane in range(3)
            for piece in (
                above[plane],
                jnp.concatenate([left[plane], own[plane]], axis=1),
                below[plane],
            )
        ],
        axis=0,
    )
    rows = 8 * PAIRS
    m_at = iota((rows, 192), 0)
    k_at = iota((rows, 192), 1)
    stored = 2 * lax.shift_right_arithmetic(m_at, 3) + (lax.shift_right_arithmetic(m_at, 2) & 1)
    plane_at = m_at & 3
    pick = (plane_at < 3) & (stored >= 1) & (stored <= 50) & (k_at == plane_at * 64 + stored + 6)
    ordered = jnp.dot(
        jnp.where(pick, 1.0, 0.0).astype(BF), stacked, preferred_element_type=F32
    ).astype(BF)
    i_at = iota((256, 256), 0) - 110
    o_at = iota((256, 256), 1)
    place_cols = jnp.where(i_at == o_at, 1.0, 0.0).astype(BF)
    laid = jnp.dot(ordered, place_cols, preferred_element_type=F32)
    for g in range(PAIRS):
        x0[:, BASE + g * STRIDE : BASE + (g + 1) * STRIDE] = laid[8 * g : 8 * g + 8, :STRIDE]

    shifts = [(pair, tap) for pair in (-1, 0, 1) for tap in range(3)]

    def narrow_columns(ref, start, width):
        pieces = [
            ref[:, start + shift_of(pair, tap) : start + shift_of(pair, tap) + width]
            for pair, tap in shifts
        ]
        return jnp.concatenate(pieces, axis=0).astype(BF)

    for start, width in tiles_of(1):
        values = lrelu(jnp.dot(w_in[...], narrow_columns(x0, start, width), preferred_element_type=F32))
        for phase in range(2):
            part = slice(32 * phase, 32 * phase + 32)
            hid[part, start : start + width] = masked(values[part], phase, start).astype(BF)
    for start, width in tiles_of(1):
        zs[:, start : start + width] = jnp.dot(
            w_out[...], hid[:, start : start + width], preferred_element_type=F32
        )
    for start, width in tiles_of(2):
        values = x0[:, start : start + width]
        for at, (pair_, tap) in enumerate(shifts):
            off = start + shift_of(pair_, tap)
            values = values + zs[8 * at : 8 * at + 8, off : off + width]
        inside = jnp.where(
            iota((8, width), 0) < 4, mask[0, :, start : start + width], mask[1, :, start : start + width]
        )
        fil[:, start : start + width] = (values * inside).astype(BF).astype(F32)

    for start, width in tiles_of(3):
        values = jnp.dot(w_first[...], narrow_columns(fil, start, width), preferred_element_type=F32)
        for phase in range(2):
            part = slice(64 * phase, 64 * phase + 64)
            xf[part, start : start + width] = masked(values[part], phase, start).astype(BF)

    def columns(ref, start, width):
        count = ref.shape[0] // 2
        pieces = []
        for phase, pair_ in SOURCE:
            for tap in range(3):
                off = start + shift_of(pair_, tap)
                pieces.append(ref[count * phase : count * (phase + 1), off : off + width])
        return jnp.concatenate(pieces, axis=0)

    for layer, (ref, weight, target) in enumerate(
        ((xf, w_f, x1), (x1, w_1, x2), (x2, w_2, x3), (x3, w_3, x4), (x4, w_4, xb))
    ):
        low = 64 * layer
        for start, width in tiles_of(4 + layer):
            span = slice(start, start + width)
            values = jnp.dot(weight[...], columns(ref, start, width), preferred_element_type=F32)
            if layer > 0:
                values = values + acc[low:, span]
            if layer < 4:
                acc[low + 64 :, span] = values[64:]
                values = lrelu(values[:64])
                count = 32
            else:
                values = xf[:, span].astype(F32) + 0.2 * values
                count = 64
            for phase in range(2):
                part = slice(count * phase, count * (phase + 1))
                target[part, span] = masked(values[part], phase, start).astype(BF)

    for start, width in tiles_of(8):
        hs[:, start : start + width] = jnp.dot(
            w_head[...], xb[:, start : start + width], preferred_element_type=F32
        )
    rows_out = []
    for g in range(5, 21):
        low = BASE + g * STRIDE
        values = None
        for at, (pair_, tap) in enumerate(shifts):
            off = low + shift_of(pair_, tap)
            term = hs[32 * at : 32 * at + 32, off : off + 256]
            values = term if values is None else values + term
        rows_out.append(values.astype(BF))
    even = jnp.concatenate([values[:16] for values in rows_out], axis=0)
    odd = jnp.concatenate([values[16:] for values in rows_out], axis=0)
    k_at = iota((256, 384), 0)
    n_at = iota((256, 384), 1)
    over = n_at - 256
    turn = jnp.where(over >= 36, over - 36, jnp.where(over >= 18, over - 18, over))
    wanted = jnp.where(over < 0, n_at, 256 + turn)
    cell = lax.shift_right_arithmetic(wanted, 1) + HALO
    spread = [
        jnp.where((k_at == cell) & ((wanted & 1) == b), 1.0, 0.0).astype(BF) for b in range(2)
    ]
    result = jnp.dot(even, spread[0], preferred_element_type=F32) + jnp.dot(
        odd, spread[1], preferred_element_type=F32
    )
    first = result[:, :128].reshape(32, 8, 128)
    second = result[:, 128:256].reshape(32, 8, 128)
    sub8 = iota((32, 8, 128), 1)
    lane8 = iota((32, 8, 128), 2)
    low8 = 18 * (sub8 & 3)
    extra = jnp.where(
        (lane8 >= low8) & (lane8 < low8 + 18), result[:, 256:].reshape(32, 8, 128), 0.0
    )
    extra = extra + pltpu.roll(extra, 1, 1) + pltpu.roll(extra, 2, 1)
    first = jnp.where((sub8 & 3) == 3, pltpu.roll(extra, 1, 1), first)
    top = sub8 < 4
    even_rows = jnp.where(top, first, pltpu.roll(second, 4, 1)).astype(BF)
    odd_rows = jnp.where(top, pltpu.roll(first, 4, 1), second).astype(BF)
    for i in range(32):
        y_ref[2 * i] = even_rows[i]
        y_ref[2 * i + 1] = odd_rows[i]


def run_main(place, left, own, above, below, pack):
    vmem = pl.BlockSpec(memory_space=pltpu.VMEM)
    return pl.pallas_call(
        main_kernel,
        out_shape=jax.ShapeDtypeStruct((64, 8, 128), BF),
        in_specs=[pl.BlockSpec(memory_space=pltpu.SMEM)] + [vmem] * 5,
        out_specs=vmem,
        scratch_shapes=[
            pltpu.VMEM((8, LANES), F32),
            pltpu.VMEM((2, 8, LANES), F32),
            pltpu.VMEM((64, LANES), BF),
            pltpu.VMEM((8, LANES), F32),
            pltpu.VMEM((128, LANES), BF),
            pltpu.VMEM((64, LANES), BF),
            pltpu.VMEM((64, LANES), BF),
            pltpu.VMEM((64, LANES), BF),
            pltpu.VMEM((64, LANES), BF),
            pltpu.VMEM((128, LANES), BF),
            pltpu.VMEM((384, LANES), F32),
            pltpu.VMEM((80, LANES), F32),
            pltpu.VMEM((288, LANES), F32),
        ],
        compiler_params=pltpu.CompilerParams(vmem_limit_bytes=44 << 20),
        cost_estimate=pl.CostEstimate(
            flops=2_000_000_000, bytes_accessed=4_000_000, transcendentals=0
        ),
        name="network",
    )(place, left, own, above, below, pack)


def edges_kernel(left, own, top, bottom):
    for target, rows in ((top, slice(0, 16)), (bottom, slice(16, 32))):
        target[:, :, :128] = left[:, rows, :]
        target[:, :, 128:] = own[:, rows, :]


def run_edges(left, own):
    vmem = pl.BlockSpec(memory_space=pltpu.VMEM)
    return pl.pallas_call(
        edges_kernel,
        out_shape=[jax.ShapeDtypeStruct((3, 16, 256), BF)] * 2,
        in_specs=[vmem] * 2,
        out_specs=[vmem] * 2,
        compiler_params=pltpu.CompilerParams(vmem_limit_bytes=8 << 20),
        name="edges",
    )(left, own)


def rows_kernel(z_ref, o_ref):
    lane = iota((4, 128), 1)
    head = lane < 110

    def halves(source):
        turned = pltpu.roll(z_ref[source].astype(F32), 110, 1)
        return turned[:4], turned[4:]

    count = z_ref.shape[0]
    first, second = halves(0)
    spare = z_ref[count - 1].astype(F32)[3:4]
    closing = jnp.concatenate(
        [pltpu.roll(spare, 110 - 18 * plane, 1) for plane in range(3)] + [spare], axis=0
    )
    for source in range(count):
        following = halves(source + 1) if source + 1 < count else (closing, None)
        at = 256 * source
        early = jnp.where(head, first, second)
        later = jnp.where(head, second, following[0])
        for plane in range(3):
            o_ref[plane, :, at : at + 128] = early[plane : plane + 1]
            o_ref[plane, :, at + 128 : at + 256] = later[plane : plane + 1]
        first, second = following


def run_rows(received):
    vmem = pl.BlockSpec(memory_space=pltpu.VMEM)
    return pl.pallas_call(
        rows_kernel,
        out_shape=jax.ShapeDtypeStruct((3, 1, 256 * received.shape[0]), F32),
        in_specs=[vmem],
        out_specs=vmem,
        compiler_params=pltpu.CompilerParams(vmem_limit_bytes=8 << 20),
        name="rows",
    )(received)


def on_device(decoded, loop_in, loop_out, first_conv, d1, d2, d3, d4, d5, head_conv):
    cols = lax.axis_size("col")
    rows = lax.axis_size("row")
    pack = run_prep(
        loop_in.transpose(0, 2, 1), loop_out, first_conv.transpose(0, 2, 1),
        d1, d2, d3, d4, d5, head_conv,
    )
    left = lax.ppermute(decoded, "col", [(i, i + 1) for i in range(cols - 1)])
    left, pack = lax.optimization_barrier((left, pack))
    top, bottom = run_edges(left, decoded)
    above = lax.ppermute(bottom, "row", [(i, i + 1) for i in range(rows - 1)])
    below = lax.ppermute(top, "row", [(i + 1, i) for i in range(rows - 1)])
    place = jnp.stack([lax.axis_index("row"), lax.axis_index("col")]).astype(jnp.int32)
    sent = run_main(place, left, decoded, above, below, pack)
    received = lax.all_to_all(sent, "col", split_axis=0, concat_axis=0, tiled=True)
    return run_rows(received).transpose(1, 0, 2)[None]


def solution(mesh):
    in_specs = (P(None, "row", "col"), P(), P(), P(), P(), P(), P(), P(), P(), P())
    out_specs = P("row", "col", None, None)
    return jax.shard_map(
        on_device, mesh=mesh, in_specs=in_specs, out_specs=out_specs, check_vma=False
    )
```

```python
import jax
import jax.numpy as jnp
from jax import lax
from jax.experimental import pallas as pl
from jax.experimental.pallas import tpu as pltpu
from jax.sharding import PartitionSpec as P

BF = jnp.bfloat16
F32 = jnp.float32

STRIDE = 147
BASE = 128
PAIRS = 26
END = BASE + PAIRS * STRIDE
LANES = 4096
STEP = 1024
HALO = 9
SOURCE = ((1, -1), (0, 0), (1, 0), (0, 1))


def shift_of(pair, tap):
    return pair * STRIDE + tap - 1


def tiles_of(layer):
    first = (layer + 1) // 2
    last = (50 - layer) // 2
    low = (BASE + first * STRIDE) // 128 * 128
    high = -(-(BASE + (last + 1) * STRIDE) // 128) * 128
    return [(start, min(STEP, high - start)) for start in range(low, high, STEP)]


def iota(shape, dim):
    return lax.broadcasted_iota(jnp.int32, shape, dim)


def place_at(pair, phase):
    return 2 * pair + phase + 1


def picking(rows, depth, entries):
    return jnp.where(entries(iota((rows, depth), 0), iota((rows, depth), 1)), 1.0, 0.0).astype(BF)


def quotient(values, by):
    return lax.shift_right_arithmetic(values * (65536 // by + 1), 16)


def sections(pack):
    return (
        pack.at[896:960, 256:328],
        pack.at[896:976, 384:448],
        pack.at[896:1024, 128:200],
        pack.at[0:384, 0:768],
        pack.at[384:704, 0:384],
        pack.at[384:640, 384:768],
        pack.at[704:896, 0:384],
        pack.at[704:832, 384:768],
        pack.at[896:1184, 0:128],
    )


BANDS = ((896, 1184), (0, 384), (384, 704), (704, 896))


def band_copies(source, target, done):
    return [
        pltpu.make_async_copy(source.at[low:high, :], target.at[low:high, :], done.at[i])
        for i, (low, high) in enumerate(BANDS)
    ]


def prep_kernel(*refs):
    given, whole, held, pack, arrived, left = refs[:9], refs[9], refs[10:19], *refs[19:22]
    targets = sections(pack)
    leaving = band_copies(pack, whole, left)
    copies = [
        pltpu.make_async_copy(source, target, arrived.at[i])
        for i, (source, target) in enumerate(zip(given, held))
    ]
    for copy in copies:
        copy.start()
    for at in (0, 1, 2, 8):
        copies[at].wait()
    loop_in, loop_out, first_conv, d1, d2, d3, d4, d5, head = held
    w_in, w_out, w_first, w_f, w_1, w_2, w_3, w_4, w_head = targets
    for source, target in ((loop_in, w_in), (first_conv, w_first)):
        outs = source.shape[2]
        blank = jnp.zeros((1, outs), F32)
        flat = jnp.concatenate(
            [piece for t in range(9) for piece in (source[t].astype(F32), blank)], axis=0
        ).astype(BF)
        sides = []
        for p in range(2):

            def entries(m, k):
                group = lax.shift_right_arithmetic(m, 3)
                pair = quotient(group, 3)
                tap = group - 3 * pair
                down = 2 * pair - 1 + (lax.shift_right_arithmetic(m, 2) & 1) - p
                ok = (down >= 0) & (down <= 2) & ((m & 3) < 3)
                return ok & (k == (down * 3 + tap) * 4 + (m & 3))

            sides.append(jnp.dot(picking(72, 36, entries), flat, preferred_element_type=F32))
        target[...] = jnp.concatenate(sides, axis=1).T.astype(BF)
    blank = jnp.zeros((1, 32), F32)
    flat = jnp.concatenate(
        [piece for t in range(9) for piece in (loop_out[t].astype(F32), blank)], axis=0
    ).astype(BF)
    sides = []
    for q in range(2):

        def entries(m, k):
            group = lax.shift_right_arithmetic(m, 3)
            pair = quotient(group, 3)
            tap = group - 3 * pair
            down = 2 * pair - 1 + q - (lax.shift_right_arithmetic(m, 2) & 1)
            ok = (down >= 0) & (down <= 2) & ((m & 3) < 3)
            return ok & (k == (down * 3 + tap) * 4 + (m & 3))

        sides.append(jnp.dot(picking(80, 36, entries), flat, preferred_element_type=F32))
    w_out[...] = jnp.concatenate(sides, axis=1).astype(BF)
    blank = jnp.zeros((4, 64), F32)
    flat = jnp.concatenate(
        [piece for t in range(9) for piece in (head[t].astype(F32), blank)], axis=0
    ).astype(BF)
    sides = []
    for q in range(2):

        def entries(m, k):
            group = lax.shift_right_arithmetic(m, 5)
            pair = quotient(group, 3)
            tap = group - 3 * pair
            b = lax.shift_right_arithmetic(m, 4) & 1
            p = lax.shift_right_arithmetic(m, 3) & 1
            a = lax.shift_right_arithmetic(m, 2) & 1
            down = 2 * pair - 1 + q - p
            ok = (down >= 0) & (down <= 2) & ((m & 3) < 3)
            return ok & (k == (down * 3 + tap) * 16 + 4 * (m & 3) + 2 * a + b)

        sides.append(jnp.dot(picking(288, 144, entries), flat, preferred_element_type=F32))
    w_head[...] = jnp.concatenate(sides, axis=1).astype(BF)
    leaving[0].start()
    for at in range(3, 8):
        copies[at].wait()
    dense = (d1, d2, d3, d4, d5)
    for source, target in enumerate((w_f, w_1, w_2, w_3, w_4)):
        low = 0 if source == 0 else 32 + 32 * source
        ins = 64 if source == 0 else 32
        row = 0
        for weight in dense[source:]:
            outs = weight.shape[1]
            taps = [weight[t, :, low : low + ins] for t in range(9)]
            none = jnp.zeros((outs, 3 * ins), BF)
            joined = jnp.concatenate(taps, axis=1)
            target[row : row + outs, :] = jnp.concatenate([joined, none], axis=1)
            target[row + outs : row + 2 * outs, :] = jnp.concatenate([none, joined], axis=1)
            row += 2 * outs
        if source in (0, 2, 4):
            leaving[1 + source // 2].start()
    for copy in leaving:
        copy.wait()


def run_prep(*weights):
    return pl.pallas_call(
        prep_kernel,
        out_shape=jax.ShapeDtypeStruct((1184, 768), BF),
        in_specs=[pl.BlockSpec(memory_space=pltpu.HBM)] * 9,
        out_specs=pl.BlockSpec(memory_space=pltpu.HBM),
        scratch_shapes=[pltpu.VMEM(weight.shape, BF) for weight in weights]
        + [
            pltpu.VMEM((1184, 768), BF),
            pltpu.SemaphoreType.DMA((9,)),
            pltpu.SemaphoreType.DMA((4,)),
        ],
        compiler_params=pltpu.CompilerParams(vmem_limit_bytes=56 << 20),
        cost_estimate=pl.CostEstimate(flops=20_000_000, bytes_accessed=3_000_000, transcendentals=0),
        name="weights",
    )(*weights)


def lrelu(values):
    return jnp.maximum(values, 0.2 * values)


def mask_kernel(place, pack, top, mask):
    row_at = place[0]
    col_at = place[1]
    lane = iota((8, LANES), 1) - BASE
    pair = lax.shift_right_arithmetic(lane * 28533, 22)
    column = lane - pair * STRIDE
    first_column = jnp.where(col_at == 0, 2 * HALO, 0)
    across = jnp.logical_and(column >= first_column, column < STRIDE - 1)
    for phase in range(2):
        row = 2 * pair + phase - 1 - HALO + 32 * row_at
        keep = jnp.logical_and(jnp.logical_and(row >= 0, row < 256), across)
        mask[phase] = jnp.where(keep, 1.0, 0.0)


def run_mask(place, pack, top):
    vmem = pl.BlockSpec(memory_space=pltpu.VMEM)
    return pl.pallas_call(
        mask_kernel,
        out_shape=jax.ShapeDtypeStruct((2, 8, LANES), F32),
        in_specs=[pl.BlockSpec(memory_space=pltpu.SMEM), vmem, vmem],
        out_specs=vmem,
        compiler_params=pltpu.CompilerParams(vmem_limit_bytes=8 << 20),
        name="mask",
    )(place, pack, top)


def main_kernel(
    mask, left, own, above, below, pack, y_ref,
    x0, hid, fil, xf, x1, x2, x3, x4, xb, acc, zs, hs,
):
    w_in, w_out, w_first, w_f, w_1, w_2, w_3, w_4, w_head = sections(pack)
    x0[:, :BASE] = jnp.zeros((8, BASE), F32)
    x0[:, END:] = jnp.zeros((8, LANES - END), F32)
    for layer, written in (
        (1, (zs,)), (2, (fil,)), (3, (xf,)), (4, (x1,)), (5, (x2,)), (6, (x3,)), (7, (x4,)), (8, (hs,))
    ):
        spans = tiles_of(layer)
        low, high = spans[0][0], spans[-1][0] + spans[-1][1]
        for ref in written:
            for side in (slice(max(low - 256, 0), low), slice(high, min(high + 256, LANES))):
                ref[:, side] = jnp.zeros((ref.shape[0], side.stop - side.start), ref.dtype)

    def masked(values, phase, start):
        rows, width = values.shape
        inside = mask[phase, :, start : start + width]
        return (values.reshape(rows // 8, 8, width) * inside[None]).reshape(rows, width)

    stacked = jnp.concatenate(
        [
            piece
            for plane in range(3)
            for piece in (
                above[plane],
                jnp.concatenate([left[plane], own[plane]], axis=1),
                below[plane],
            )
        ],
        axis=0,
    )
    rows = 8 * PAIRS
    m_at = iota((rows, 192), 0)
    k_at = iota((rows, 192), 1)
    stored = 2 * lax.shift_right_arithmetic(m_at, 3) + (lax.shift_right_arithmetic(m_at, 2) & 1)
    plane_at = m_at & 3
    pick = (plane_at < 3) & (stored >= 1) & (stored <= 50) & (k_at == plane_at * 64 + stored + 6)
    ordered = jnp.dot(
        jnp.where(pick, 1.0, 0.0).astype(BF), stacked, preferred_element_type=F32
    ).astype(BF)
    i_at = iota((256, 256), 0) - 110
    o_at = iota((256, 256), 1)
    place_cols = jnp.where(i_at == o_at, 1.0, 0.0).astype(BF)
    laid = jnp.dot(ordered, place_cols, preferred_element_type=F32)
    for g in range(PAIRS):
        x0[:, BASE + g * STRIDE : BASE + (g + 1) * STRIDE] = laid[8 * g : 8 * g + 8, :STRIDE]

    shifts = [(pair, tap) for pair in (-1, 0, 1) for tap in range(3)]

    def narrow_columns(ref, start, width):
        pieces = [
            ref[:, start + shift_of(pair, tap) : start + shift_of(pair, tap) + width]
            for pair, tap in shifts
        ]
        return jnp.concatenate(pieces, axis=0).astype(BF)

    for start, width in tiles_of(1):
        values = lrelu(jnp.dot(w_in[...], narrow_columns(x0, start, width), preferred_element_type=F32))
        for phase in range(2):
            part = slice(32 * phase, 32 * phase + 32)
            hid[part, start : start + width] = masked(values[part], phase, start).astype(BF)
    for start, width in tiles_of(1):
        zs[:, start : start + width] = jnp.dot(
            w_out[...], hid[:, start : start + width], preferred_element_type=F32
        )
    for start, width in tiles_of(2):
        values = x0[:, start : start + width]
        for at, (pair_, tap) in enumerate(shifts):
            off = start + shift_of(pair_, tap)
            values = values + zs[8 * at : 8 * at + 8, off : off + width]
        inside = jnp.where(
            iota((8, width), 0) < 4, mask[0, :, start : start + width], mask[1, :, start : start + width]
        )
        fil[:, start : start + width] = (values * inside).astype(BF).astype(F32)

    for start, width in tiles_of(3):
        values = jnp.dot(w_first[...], narrow_columns(fil, start, width), preferred_element_type=F32)
        for phase in range(2):
            part = slice(64 * phase, 64 * phase + 64)
            xf[part, start : start + width] = masked(values[part], phase, start).astype(BF)

    def columns(ref, start, width):
        count = ref.shape[0] // 2
        pieces = []
        for phase, pair_ in SOURCE:
            for tap in range(3):
                off = start + shift_of(pair_, tap)
                pieces.append(ref[count * phase : count * (phase + 1), off : off + width])
        return jnp.concatenate(pieces, axis=0)

    for layer, (ref, weight, target) in enumerate(
        ((xf, w_f, x1), (x1, w_1, x2), (x2, w_2, x3), (x3, w_3, x4), (x4, w_4, xb))
    ):
        low = 64 * layer
        for start, width in tiles_of(4 + layer):
            span = slice(start, start + width)
            values = jnp.dot(weight[...], columns(ref, start, width), preferred_element_type=F32)
            if layer > 0:
                values = values + acc[low:, span]
            if layer < 4:
                acc[low + 64 :, span] = values[64:]
                values = lrelu(values[:64])
                count = 32
            else:
                values = xf[:, span].astype(F32) + 0.2 * values
                count = 64
            for phase in range(2):
                part = slice(count * phase, count * (phase + 1))
                target[part, span] = masked(values[part], phase, start).astype(BF)

    for start, width in tiles_of(8):
        hs[:, start : start + width] = jnp.dot(
            w_head[...], xb[:, start : start + width], preferred_element_type=F32
        )
    rows_out = []
    for g in range(5, 21):
        low = BASE + g * STRIDE
        values = None
        for at, (pair_, tap) in enumerate(shifts):
            off = low + shift_of(pair_, tap)
            term = hs[32 * at : 32 * at + 32, off : off + 256]
            values = term if values is None else values + term
        rows_out.append(values.astype(BF))
    even = jnp.concatenate([values[:16] for values in rows_out], axis=0)
    odd = jnp.concatenate([values[16:] for values in rows_out], axis=0)
    k_at = iota((256, 384), 0)
    n_at = iota((256, 384), 1)
    over = n_at - 256
    turn = jnp.where(over >= 36, over - 36, jnp.where(over >= 18, over - 18, over))
    wanted = jnp.where(over < 0, n_at, 256 + turn)
    cell = lax.shift_right_arithmetic(wanted, 1) + HALO
    spread = [
        jnp.where((k_at == cell) & ((wanted & 1) == b), 1.0, 0.0).astype(BF) for b in range(2)
    ]
    result = jnp.dot(even, spread[0], preferred_element_type=F32) + jnp.dot(
        odd, spread[1], preferred_element_type=F32
    )
    first = result[:, :128].reshape(32, 8, 128)
    second = result[:, 128:256].reshape(32, 8, 128)
    sub8 = iota((32, 8, 128), 1)
    lane8 = iota((32, 8, 128), 2)
    low8 = 18 * (sub8 & 3)
    extra = jnp.where(
        (lane8 >= low8) & (lane8 < low8 + 18), result[:, 256:].reshape(32, 8, 128), 0.0
    )
    extra = extra + pltpu.roll(extra, 1, 1) + pltpu.roll(extra, 2, 1)
    first = jnp.where((sub8 & 3) == 3, pltpu.roll(extra, 1, 1), first)
    top = sub8 < 4
    even_rows = jnp.where(top, first, pltpu.roll(second, 4, 1)).astype(BF)
    odd_rows = jnp.where(top, pltpu.roll(first, 4, 1), second).astype(BF)
    for i in range(32):
        y_ref[2 * i] = even_rows[i]
        y_ref[2 * i + 1] = odd_rows[i]


def run_main(mask, left, own, above, below, pack):
    vmem = pl.BlockSpec(memory_space=pltpu.VMEM)
    return pl.pallas_call(
        main_kernel,
        out_shape=jax.ShapeDtypeStruct((64, 8, 128), BF),
        in_specs=[vmem] * 6,
        out_specs=vmem,
        scratch_shapes=[
            pltpu.VMEM((8, LANES), F32),
            pltpu.VMEM((64, LANES), BF),
            pltpu.VMEM((8, LANES), F32),
            pltpu.VMEM((128, LANES), BF),
            pltpu.VMEM((64, LANES), BF),
            pltpu.VMEM((64, LANES), BF),
            pltpu.VMEM((64, LANES), BF),
            pltpu.VMEM((64, LANES), BF),
            pltpu.VMEM((128, LANES), BF),
            pltpu.VMEM((384, LANES), F32),
            pltpu.VMEM((80, LANES), F32),
            pltpu.VMEM((288, LANES), F32),
        ],
        compiler_params=pltpu.CompilerParams(vmem_limit_bytes=44 << 20),
        cost_estimate=pl.CostEstimate(
            flops=2_000_000_000, bytes_accessed=4_000_000, transcendentals=0
        ),
        name="network",
    )(mask, left, own, above, below, pack)


def edges_kernel(left, own, top, bottom):
    for target, rows in ((top, slice(0, 16)), (bottom, slice(16, 32))):
        target[:, :, :128] = left[:, rows, :]
        target[:, :, 128:] = own[:, rows, :]


def run_edges(left, own):
    vmem = pl.BlockSpec(memory_space=pltpu.VMEM)
    return pl.pallas_call(
        edges_kernel,
        out_shape=[jax.ShapeDtypeStruct((3, 16, 256), BF)] * 2,
        in_specs=[vmem] * 2,
        out_specs=[vmem] * 2,
        compiler_params=pltpu.CompilerParams(vmem_limit_bytes=8 << 20),
        name="edges",
    )(left, own)


def rows_kernel(z_ref, o_ref):
    lane = iota((4, 128), 1)
    head = lane < 110

    def halves(source):
        turned = pltpu.roll(z_ref[source].astype(F32), 110, 1)
        return turned[:4], turned[4:]

    count = z_ref.shape[0]
    first, second = halves(0)
    spare = z_ref[count - 1].astype(F32)[3:4]
    closing = jnp.concatenate(
        [pltpu.roll(spare, 110 - 18 * plane, 1) for plane in range(3)] + [spare], axis=0
    )
    for source in range(count):
        following = halves(source + 1) if source + 1 < count else (closing, None)
        at = 256 * source
        early = jnp.where(head, first, second)
        later = jnp.where(head, second, following[0])
        for plane in range(3):
            o_ref[plane, :, at : at + 128] = early[plane : plane + 1]
            o_ref[plane, :, at + 128 : at + 256] = later[plane : plane + 1]
        first, second = following


def run_rows(received):
    vmem = pl.BlockSpec(memory_space=pltpu.VMEM)
    return pl.pallas_call(
        rows_kernel,
        out_shape=jax.ShapeDtypeStruct((3, 1, 256 * received.shape[0]), F32),
        in_specs=[vmem],
        out_specs=vmem,
        compiler_params=pltpu.CompilerParams(vmem_limit_bytes=8 << 20),
        name="rows",
    )(received)


def on_device(decoded, loop_in, loop_out, first_conv, d1, d2, d3, d4, d5, head_conv):
    cols = lax.axis_size("col")
    rows = lax.axis_size("row")
    pack = run_prep(
        loop_in.transpose(0, 2, 1), loop_out, first_conv.transpose(0, 2, 1),
        d1, d2, d3, d4, d5, head_conv,
    )
    left = lax.ppermute(decoded, "col", [(i, i + 1) for i in range(cols - 1)])
    left, pack = lax.optimization_barrier((left, pack))
    top, bottom = run_edges(left, decoded)
    above = lax.ppermute(bottom, "row", [(i, i + 1) for i in range(rows - 1)])
    below = lax.ppermute(top, "row", [(i + 1, i) for i in range(rows - 1)])
    place = jnp.stack([lax.axis_index("row"), lax.axis_index("col")]).astype(jnp.int32)
    mask = run_mask(place, pack, top)
    sent = run_main(mask, left, decoded, above, below, pack)
    received = lax.all_to_all(sent, "col", split_axis=0, concat_axis=0, tiled=True)
    return run_rows(received).transpose(1, 0, 2)[None]


def solution(mesh):
    in_specs = (P(None, "row", "col"), P(), P(), P(), P(), P(), P(), P(), P(), P())
    out_specs = P("row", "col", None, None)
    return jax.shard_map(
        on_device, mesh=mesh, in_specs=in_specs, out_specs=out_specs, check_vma=False
    )
```

```python
import jax
import jax.numpy as jnp
from jax import lax
from jax.experimental import pallas as pl
from jax.experimental.pallas import tpu as pltpu
from jax.sharding import PartitionSpec as P

BF = jnp.bfloat16
F32 = jnp.float32

STRIDE = 147
BASE = 128
PAIRS = 26
END = BASE + PAIRS * STRIDE
LANES = 4096
STEP = 1280
HALO = 9
SOURCE = ((1, -1), (0, 0), (1, 0), (0, 1))


def shift_of(pair, tap):
    return pair * STRIDE + tap - 1


def tiles_of(layer):
    first = (layer + 1) // 2
    last = (50 - layer) // 2
    low = (BASE + first * STRIDE) // 128 * 128
    high = -(-(BASE + (last + 1) * STRIDE) // 128) * 128
    return [(start, min(STEP, high - start)) for start in range(low, high, STEP)]


def iota(shape, dim):
    return lax.broadcasted_iota(jnp.int32, shape, dim)


def place_at(pair, phase):
    return 2 * pair + phase + 1


def picking(rows, depth, entries):
    return jnp.where(entries(iota((rows, depth), 0), iota((rows, depth), 1)), 1.0, 0.0).astype(BF)


def quotient(values, by):
    return lax.shift_right_arithmetic(values * (65536 // by + 1), 16)


def sections(pack):
    return (
        pack.at[896:960, 256:328],
        pack.at[896:976, 384:448],
        pack.at[896:1024, 128:200],
        pack.at[0:384, 0:768],
        pack.at[384:704, 0:384],
        pack.at[384:640, 384:768],
        pack.at[704:896, 0:384],
        pack.at[704:832, 384:768],
        pack.at[896:1184, 0:128],
    )


BANDS = ((896, 1184), (0, 384), (384, 704), (704, 896))


def band_copies(source, target, done):
    return [
        pltpu.make_async_copy(source.at[low:high, :], target.at[low:high, :], done.at[i])
        for i, (low, high) in enumerate(BANDS)
    ]


def prep_kernel(*refs):
    given, whole, held, pack, arrived, left = refs[:9], refs[9], refs[10:19], *refs[19:22]
    targets = sections(pack)
    leaving = band_copies(pack, whole, left)
    copies = [
        pltpu.make_async_copy(source, target, arrived.at[i])
        for i, (source, target) in enumerate(zip(given, held))
    ]
    for copy in copies:
        copy.start()
    for at in (0, 1, 2, 8):
        copies[at].wait()
    loop_in, loop_out, first_conv, d1, d2, d3, d4, d5, head = held
    w_in, w_out, w_first, w_f, w_1, w_2, w_3, w_4, w_head = targets
    for source, target in ((loop_in, w_in), (first_conv, w_first)):
        outs = source.shape[2]
        blank = jnp.zeros((1, outs), F32)
        flat = jnp.concatenate(
            [piece for t in range(9) for piece in (source[t].astype(F32), blank)], axis=0
        ).astype(BF)
        sides = []
        for p in range(2):

            def entries(m, k):
                group = lax.shift_right_arithmetic(m, 3)
                pair = quotient(group, 3)
                tap = group - 3 * pair
                down = 2 * pair - 1 + (lax.shift_right_arithmetic(m, 2) & 1) - p
                ok = (down >= 0) & (down <= 2) & ((m & 3) < 3)
                return ok & (k == (down * 3 + tap) * 4 + (m & 3))

            sides.append(jnp.dot(picking(72, 36, entries), flat, preferred_element_type=F32))
        target[...] = jnp.concatenate(sides, axis=1).T.astype(BF)
    blank = jnp.zeros((1, 32), F32)
    flat = jnp.concatenate(
        [piece for t in range(9) for piece in (loop_out[t].astype(F32), blank)], axis=0
    ).astype(BF)
    sides = []
    for q in range(2):

        def entries(m, k):
            group = lax.shift_right_arithmetic(m, 3)
            pair = quotient(group, 3)
            tap = group - 3 * pair
            down = 2 * pair - 1 + q - (lax.shift_right_arithmetic(m, 2) & 1)
            ok = (down >= 0) & (down <= 2) & ((m & 3) < 3)
            return ok & (k == (down * 3 + tap) * 4 + (m & 3))

        sides.append(jnp.dot(picking(80, 36, entries), flat, preferred_element_type=F32))
    w_out[...] = jnp.concatenate(sides, axis=1).astype(BF)
    blank = jnp.zeros((4, 64), F32)
    flat = jnp.concatenate(
        [piece for t in range(9) for piece in (head[t].astype(F32), blank)], axis=0
    ).astype(BF)
    sides = []
    for q in range(2):

        def entries(m, k):
            group = lax.shift_right_arithmetic(m, 5)
            pair = quotient(group, 3)
            tap = group - 3 * pair
            b = lax.shift_right_arithmetic(m, 4) & 1
            p = lax.shift_right_arithmetic(m, 3) & 1
            a = lax.shift_right_arithmetic(m, 2) & 1
            down = 2 * pair - 1 + q - p
            ok = (down >= 0) & (down <= 2) & ((m & 3) < 3)
            return ok & (k == (down * 3 + tap) * 16 + 4 * (m & 3) + 2 * a + b)

        sides.append(jnp.dot(picking(288, 144, entries), flat, preferred_element_type=F32))
    w_head[...] = jnp.concatenate(sides, axis=1).astype(BF)
    leaving[0].start()
    for at in range(3, 8):
        copies[at].wait()
    dense = (d1, d2, d3, d4, d5)
    for source, target in enumerate((w_f, w_1, w_2, w_3, w_4)):
        low = 0 if source == 0 else 32 + 32 * source
        ins = 64 if source == 0 else 32
        row = 0
        for weight in dense[source:]:
            outs = weight.shape[1]
            taps = [weight[t, :, low : low + ins] for t in range(9)]
            none = jnp.zeros((outs, 3 * ins), BF)
            joined = jnp.concatenate(taps, axis=1)
            target[row : row + outs, :] = jnp.concatenate([joined, none], axis=1)
            target[row + outs : row + 2 * outs, :] = jnp.concatenate([none, joined], axis=1)
            row += 2 * outs
        if source in (0, 2, 4):
            leaving[1 + source // 2].start()
    for copy in leaving:
        copy.wait()


def run_prep(*weights):
    return pl.pallas_call(
        prep_kernel,
        out_shape=jax.ShapeDtypeStruct((1184, 768), BF),
        in_specs=[pl.BlockSpec(memory_space=pltpu.HBM)] * 9,
        out_specs=pl.BlockSpec(memory_space=pltpu.HBM),
        scratch_shapes=[pltpu.VMEM(weight.shape, BF) for weight in weights]
        + [
            pltpu.VMEM((1184, 768), BF),
            pltpu.SemaphoreType.DMA((9,)),
            pltpu.SemaphoreType.DMA((4,)),
        ],
        compiler_params=pltpu.CompilerParams(vmem_limit_bytes=56 << 20),
        cost_estimate=pl.CostEstimate(flops=20_000_000, bytes_accessed=3_000_000, transcendentals=0),
        name="weights",
    )(*weights)


def lrelu(values):
    return jnp.maximum(values, 0.2 * values)


def mask_kernel(place, pack, top, mask):
    row_at = place[0]
    col_at = place[1]
    lane = iota((8, LANES), 1) - BASE
    pair = lax.shift_right_arithmetic(lane * 28533, 22)
    column = lane - pair * STRIDE
    first_column = jnp.where(col_at == 0, 2 * HALO, 0)
    across = jnp.logical_and(column >= first_column, column < STRIDE - 1)
    for phase in range(2):
        row = 2 * pair + phase - 1 - HALO + 32 * row_at
        keep = jnp.logical_and(jnp.logical_and(row >= 0, row < 256), across)
        mask[phase] = jnp.where(keep, 1.0, 0.0)


def run_mask(place, pack, top):
    vmem = pl.BlockSpec(memory_space=pltpu.VMEM)
    return pl.pallas_call(
        mask_kernel,
        out_shape=jax.ShapeDtypeStruct((2, 8, LANES), F32),
        in_specs=[pl.BlockSpec(memory_space=pltpu.SMEM), vmem, vmem],
        out_specs=vmem,
        compiler_params=pltpu.CompilerParams(vmem_limit_bytes=8 << 20),
        name="mask",
    )(place, pack, top)


def main_kernel(
    mask, left, own, above, below, pack, y_ref,
    x0, hid, fil, xf, x1, x2, x3, x4, xb, acc, zs, hs,
):
    w_in, w_out, w_first, w_f, w_1, w_2, w_3, w_4, w_head = sections(pack)
    x0[:, :BASE] = jnp.zeros((8, BASE), F32)
    x0[:, END:] = jnp.zeros((8, LANES - END), F32)
    for layer, written in (
        (1, (zs,)), (2, (fil,)), (3, (xf,)), (4, (x1,)), (5, (x2,)), (6, (x3,)), (7, (x4,)), (8, (hs,))
    ):
        spans = tiles_of(layer)
        low, high = spans[0][0], spans[-1][0] + spans[-1][1]
        for ref in written:
            for side in (slice(max(low - 256, 0), low), slice(high, min(high + 256, LANES))):
                ref[:, side] = jnp.zeros((ref.shape[0], side.stop - side.start), ref.dtype)

    def masked(values, phase, start):
        rows, width = values.shape
        inside = mask[phase, :, start : start + width]
        return (values.reshape(rows // 8, 8, width) * inside[None]).reshape(rows, width)

    stacked = jnp.concatenate(
        [
            piece
            for plane in range(3)
            for piece in (
                above[plane],
                jnp.concatenate([left[plane], own[plane]], axis=1),
                below[plane],
            )
        ],
        axis=0,
    )
    rows = 8 * PAIRS
    m_at = iota((rows, 192), 0)
    k_at = iota((rows, 192), 1)
    stored = 2 * lax.shift_right_arithmetic(m_at, 3) + (lax.shift_right_arithmetic(m_at, 2) & 1)
    plane_at = m_at & 3
    pick = (plane_at < 3) & (stored >= 1) & (stored <= 50) & (k_at == plane_at * 64 + stored + 6)
    ordered = jnp.dot(
        jnp.where(pick, 1.0, 0.0).astype(BF), stacked, preferred_element_type=F32
    ).astype(BF)
    i_at = iota((256, 256), 0) - 110
    o_at = iota((256, 256), 1)
    place_cols = jnp.where(i_at == o_at, 1.0, 0.0).astype(BF)
    laid = jnp.dot(ordered, place_cols, preferred_element_type=F32)
    for g in range(PAIRS):
        x0[:, BASE + g * STRIDE : BASE + (g + 1) * STRIDE] = laid[8 * g : 8 * g + 8, :STRIDE]

    shifts = [(pair, tap) for pair in (-1, 0, 1) for tap in range(3)]

    def narrow_columns(ref, start, width):
        pieces = [
            ref[:, start + shift_of(pair, tap) : start + shift_of(pair, tap) + width]
            for pair, tap in shifts
        ]
        return jnp.concatenate(pieces, axis=0).astype(BF)

    for start, width in tiles_of(1):
        values = lrelu(jnp.dot(w_in[...], narrow_columns(x0, start, width), preferred_element_type=F32))
        for phase in range(2):
            part = slice(32 * phase, 32 * phase + 32)
            hid[part, start : start + width] = masked(values[part], phase, start).astype(BF)
    for start, width in tiles_of(1):
        zs[:, start : start + width] = jnp.dot(
            w_out[...], hid[:, start : start + width], preferred_element_type=F32
        )
    for start, width in tiles_of(2):
        values = x0[:, start : start + width]
        for at, (pair_, tap) in enumerate(shifts):
            off = start + shift_of(pair_, tap)
            values = values + zs[8 * at : 8 * at + 8, off : off + width]
        inside = jnp.where(
            iota((8, width), 0) < 4, mask[0, :, start : start + width], mask[1, :, start : start + width]
        )
        fil[:, start : start + width] = (values * inside).astype(BF).astype(F32)

    for start, width in tiles_of(3):
        values = jnp.dot(w_first[...], narrow_columns(fil, start, width), preferred_element_type=F32)
        for phase in range(2):
            part = slice(64 * phase, 64 * phase + 64)
            xf[part, start : start + width] = masked(values[part], phase, start).astype(BF)

    def columns(ref, start, width):
        count = ref.shape[0] // 2
        pieces = []
        for phase, pair_ in SOURCE:
            for tap in range(3):
                off = start + shift_of(pair_, tap)
                pieces.append(ref[count * phase : count * (phase + 1), off : off + width])
        return jnp.concatenate(pieces, axis=0)

    for layer, (ref, weight, target) in enumerate(
        ((xf, w_f, x1), (x1, w_1, x2), (x2, w_2, x3), (x3, w_3, x4), (x4, w_4, xb))
    ):
        low = 64 * layer
        for start, width in tiles_of(4 + layer):
            span = slice(start, start + width)
            values = jnp.dot(weight[...], columns(ref, start, width), preferred_element_type=F32)
            if layer > 0:
                values = values + acc[low:, span]
            if layer < 4:
                acc[low + 64 :, span] = values[64:]
                values = lrelu(values[:64])
                count = 32
            else:
                values = xf[:, span].astype(F32) + 0.2 * values
                count = 64
            for phase in range(2):
                part = slice(count * phase, count * (phase + 1))
                target[part, span] = masked(values[part], phase, start).astype(BF)

    for start, width in tiles_of(8):
        hs[:, start : start + width] = jnp.dot(
            w_head[...], xb[:, start : start + width], preferred_element_type=F32
        )
    rows_out = []
    for g in range(5, 21):
        low = BASE + g * STRIDE
        values = None
        for at, (pair_, tap) in enumerate(shifts):
            off = low + shift_of(pair_, tap)
            term = hs[32 * at : 32 * at + 32, off : off + 256]
            values = term if values is None else values + term
        rows_out.append(values.astype(BF))
    even = jnp.concatenate([values[:16] for values in rows_out], axis=0)
    odd = jnp.concatenate([values[16:] for values in rows_out], axis=0)
    k_at = iota((256, 384), 0)
    n_at = iota((256, 384), 1)
    over = n_at - 256
    turn = jnp.where(over >= 36, over - 36, jnp.where(over >= 18, over - 18, over))
    wanted = jnp.where(over < 0, n_at, 256 + turn)
    cell = lax.shift_right_arithmetic(wanted, 1) + HALO
    spread = [
        jnp.where((k_at == cell) & ((wanted & 1) == b), 1.0, 0.0).astype(BF) for b in range(2)
    ]
    result = jnp.dot(even, spread[0], preferred_element_type=F32) + jnp.dot(
        odd, spread[1], preferred_element_type=F32
    )
    first = result[:, :128].reshape(32, 8, 128)
    second = result[:, 128:256].reshape(32, 8, 128)
    sub8 = iota((32, 8, 128), 1)
    lane8 = iota((32, 8, 128), 2)
    low8 = 18 * (sub8 & 3)
    extra = jnp.where(
        (lane8 >= low8) & (lane8 < low8 + 18), result[:, 256:].reshape(32, 8, 128), 0.0
    )
    extra = extra + pltpu.roll(extra, 1, 1) + pltpu.roll(extra, 2, 1)
    first = jnp.where((sub8 & 3) == 3, pltpu.roll(extra, 1, 1), first)
    top = sub8 < 4
    even_rows = jnp.where(top, first, pltpu.roll(second, 4, 1)).astype(BF)
    odd_rows = jnp.where(top, pltpu.roll(first, 4, 1), second).astype(BF)
    for i in range(32):
        y_ref[2 * i] = even_rows[i]
        y_ref[2 * i + 1] = odd_rows[i]


def run_main(mask, left, own, above, below, pack):
    vmem = pl.BlockSpec(memory_space=pltpu.VMEM)
    return pl.pallas_call(
        main_kernel,
        out_shape=jax.ShapeDtypeStruct((64, 8, 128), BF),
        in_specs=[vmem] * 6,
        out_specs=vmem,
        scratch_shapes=[
            pltpu.VMEM((8, LANES), F32),
            pltpu.VMEM((64, LANES), BF),
            pltpu.VMEM((8, LANES), F32),
            pltpu.VMEM((128, LANES), BF),
            pltpu.VMEM((64, LANES), BF),
            pltpu.VMEM((64, LANES), BF),
            pltpu.VMEM((64, LANES), BF),
            pltpu.VMEM((64, LANES), BF),
            pltpu.VMEM((128, LANES), BF),
            pltpu.VMEM((384, LANES), F32),
            pltpu.VMEM((80, LANES), F32),
            pltpu.VMEM((288, LANES), F32),
        ],
        compiler_params=pltpu.CompilerParams(vmem_limit_bytes=44 << 20),
        cost_estimate=pl.CostEstimate(
            flops=2_000_000_000, bytes_accessed=4_000_000, transcendentals=0
        ),
        name="network",
    )(mask, left, own, above, below, pack)


def edges_kernel(left, own, top, bottom):
    for target, rows in ((top, slice(0, 16)), (bottom, slice(16, 32))):
        target[:, :, :128] = left[:, rows, :]
        target[:, :, 128:] = own[:, rows, :]


def run_edges(left, own):
    vmem = pl.BlockSpec(memory_space=pltpu.VMEM)
    return pl.pallas_call(
        edges_kernel,
        out_shape=[jax.ShapeDtypeStruct((3, 16, 256), BF)] * 2,
        in_specs=[vmem] * 2,
        out_specs=[vmem] * 2,
        compiler_params=pltpu.CompilerParams(vmem_limit_bytes=8 << 20),
        name="edges",
    )(left, own)


def rows_kernel(z_ref, o_ref):
    lane = iota((4, 128), 1)
    head = lane < 110

    def halves(source):
        turned = pltpu.roll(z_ref[source].astype(F32), 110, 1)
        return turned[:4], turned[4:]

    count = z_ref.shape[0]
    first, second = halves(0)
    spare = z_ref[count - 1].astype(F32)[3:4]
    closing = jnp.concatenate(
        [pltpu.roll(spare, 110 - 18 * plane, 1) for plane in range(3)] + [spare], axis=0
    )
    for source in range(count):
        following = halves(source + 1) if source + 1 < count else (closing, None)
        at = 256 * source
        early = jnp.where(head, first, second)
        later = jnp.where(head, second, following[0])
        for plane in range(3):
            o_ref[plane, :, at : at + 128] = early[plane : plane + 1]
            o_ref[plane, :, at + 128 : at + 256] = later[plane : plane + 1]
        first, second = following


def run_rows(received):
    vmem = pl.BlockSpec(memory_space=pltpu.VMEM)
    return pl.pallas_call(
        rows_kernel,
        out_shape=jax.ShapeDtypeStruct((3, 1, 256 * received.shape[0]), F32),
        in_specs=[vmem],
        out_specs=vmem,
        compiler_params=pltpu.CompilerParams(vmem_limit_bytes=8 << 20),
        name="rows",
    )(received)


def on_device(decoded, loop_in, loop_out, first_conv, d1, d2, d3, d4, d5, head_conv):
    cols = lax.axis_size("col")
    rows = lax.axis_size("row")
    pack = run_prep(
        loop_in.transpose(0, 2, 1), loop_out, first_conv.transpose(0, 2, 1),
        d1, d2, d3, d4, d5, head_conv,
    )
    left = lax.ppermute(decoded, "col", [(i, i + 1) for i in range(cols - 1)])
    left, pack = lax.optimization_barrier((left, pack))
    top, bottom = run_edges(left, decoded)
    above = lax.ppermute(bottom, "row", [(i, i + 1) for i in range(rows - 1)])
    below = lax.ppermute(top, "row", [(i + 1, i) for i in range(rows - 1)])
    place = jnp.stack([lax.axis_index("row"), lax.axis_index("col")]).astype(jnp.int32)
    mask = run_mask(place, pack, top)
    sent = run_main(mask, left, decoded, above, below, pack)
    received = lax.all_to_all(sent, "col", split_axis=0, concat_axis=0, tiled=True)
    return run_rows(received).transpose(1, 0, 2)[None]


def solution(mesh):
    in_specs = (P(None, "row", "col"), P(), P(), P(), P(), P(), P(), P(), P(), P())
    out_specs = P("row", "col", None, None)
    return jax.shard_map(
        on_device, mesh=mesh, in_specs=in_specs, out_specs=out_specs, check_vma=False
    )
```
